512 devices in a mesh: event: 16 (over y, core), cuts: 32 (over z, x).
Axes of the slice: x: 4, y: 8, z: 8, core: 2. Of those that a mesh axis runs over, the one named last changes fastest.
Arguments:
- point_traces: bfloat16 [3072, 3, 25, 2048], P(('event', 'cuts')), parts along dimension 0, may hold values from -6 to 6
- rec_element: int32 [16384], P(('event', 'cuts')), parts along dimension 0, may hold values from 0 to 5
- rec_coords: float32 [2, 16384], P(None, ('event', 'cuts')), parts along dimension 1, may hold values from -0.95 to 0.95
- slot_block: int32 [16384, 1], P(('event', 'cuts')), parts along dimension 0, may hold values from 0 to 31; in each aligned block of 32 rows (0 to 31, 32 to 63, ...) at most 2 rows name the same one
- window_start: int32 [16384], P(('event', 'cuts')), parts along dimension 0, may hold values from 0 to 1024
- window_end: int32 [16384], P(('event', 'cuts')), parts along dimension 0, may hold values from 256 to 2048, as said below
- obs_windows: bfloat16 [32768, 3, 1024], P(('event', 'cuts')), parts along dimension 0, may hold values from -6 to 6
Outputs:
- adj_points: bfloat16 [3072, 3, 25, 2048], P(('event', 'cuts')), parts along dimension 0
- total_misfit: float32 [16], P('event'), parts along dimension 0
The draws below stay inside these ranges and needn't reach their ends.
There are 16 independent parts, one for each index of `event`. The reference program is written for one: setup_inputs(seed, part) draws one part's arguments, and reference() takes and returns one part's arrays. A program takes and returns all parts, laid end to end along the dimension named above; each array names one. Nothing has to cross between parts.
Inputs may be any that keep to these rules, and one draw needn't show every extreme that they name: `slot_block`: among the receivers of one slice at most 2 have one block; some block has exactly 2 of them. window_end - window_start lies in [256, 1024] and equals 1024 for some station.
All inputs are finite; a program needn't handle non-finite values.
Results may differ from the reference program's by a relative error of at most 0.0057.
Values may be sent and summed in bfloat16 or wider, within the bound.
No kernel may reach another device: no remote copies, remote signals or barrier semaphores. Data moves between devices by JAX's collectives and lax.ppermute only.
A program may use at most 64 MiB of HBM per device.

```python
import math
import jax
import jax.numpy as jnp
import numpy as np
from jax import lax

ELEM_DEV = 6
R_DEV = 32
NT = 2048
WIN = 1024
WMIN = 256
TAPERS = 5
FACE = 25
NF = 512
CAP = 2
STATIONS = 1024
ELEMS = 192
N_CUTS = 32


def window_pair(key):
    key = jax.random.fold_in(key, 11)
    first_key, second_key, third_key = jax.random.split(key, 3)
    lengths = jax.random.randint(first_key, (STATIONS,), WMIN, WIN + 1)
    longest = jax.random.randint(second_key, (), 0, STATIONS)
    lengths = jnp.where(jnp.arange(STATIONS) == longest, WIN, lengths)
    starts = jax.random.randint(third_key, (STATIONS,), 0, NT - WIN + 1)
    return (starts.astype(jnp.int32), (starts + lengths).astype(jnp.int32))


def draw_window_start(key, part):
    return window_pair(key)[0]


def draw_window_end(key, part):
    return window_pair(key)[1]


def touch_ends(values, key, low, high):
    index_at = [jax.random.randint(jax.random.fold_in(key, axis), (), 0, length) for axis, length in enumerate(values.shape)]
    main_axis = values.shape.index(max(values.shape))
    next_to = index_at[:main_axis] + [(index_at[main_axis] + 1) % values.shape[main_axis]] + index_at[main_axis + 1:]
    return values.at[tuple(index_at)].set(low).at[tuple(next_to)].set(high)


def levels(own_key, shape, pieces, smallest, largest):
    def one(axis_at, parts):
        steps = jax.random.uniform(jax.random.fold_in(jax.random.fold_in(own_key, 6), axis_at), (parts,), jnp.float32, smallest / len(pieces), largest / len(pieces))
        return jnp.repeat(jnp.exp(steps), shape[axis_at] // parts).reshape((-1,) + (1,) * (len(shape) - axis_at - 1))

    level = one(*pieces[0])
    for cut in pieces[1:]:
        level = level * one(*cut)
    return level


def deal_out(stream_key, own, number, rows, amount, top, most, skew):
    sequence = jax.random.permutation(stream_key, amount)
    crowded, common = portions_of(amount, rows * top, most, skew, True), portions_of(amount, rows * top, most, skew, False)
    places = jnp.arange(amount)

    def named(tallies, turn):
        used = int((tallies > 0).sum())
        fixed = max(1, used // 4)
        moved = fixed + (places - fixed + turn * (used - fixed)) % max(1, amount - fixed)
        return jnp.zeros((amount,), jnp.int32).at[sequence[jnp.where(places < fixed, places, moved)]].set(jnp.asarray(tallies, jnp.int32))

    tallies = jnp.where(number % 4 == 0, named(crowded, number // 4), named(common, number - number // 4 - 1))
    mixed = jax.random.permutation(jax.random.fold_in(own, 3), amount)
    giver, taker = mixed[0:amount // 2 * 2:2], mixed[1:amount // 2 * 2:2]
    margin = jnp.minimum(tallies[giver] - 1, most - tallies[taker]) // 2
    margin = jnp.where((giver == sequence[0]) | (taker == sequence[0]) | (tallies[taker] == 0), 0, jnp.maximum(margin, 0))
    moved = jax.random.randint(jax.random.fold_in(own, 4), (amount // 2,), 0, 1 << 20) % (margin + 1)
    tallies = tallies.at[giver].add(-moved).at[taker].add(moved)
    items = jnp.searchsorted(jnp.cumsum(tallies), jnp.arange(rows * top), side="right").astype(jnp.int32)
    grid = items.reshape(top, rows).T
    grid = grid[jax.random.permutation(jax.random.fold_in(own, 1), rows)]
    turn = jax.random.randint(jax.random.fold_in(own, 2), (rows, 1), 0, top)
    return jnp.take_along_axis(grid, (jnp.arange(top)[None, :] + turn) % top, axis=1)


def portions_of(count, total, bound, lean, full):
    weights = [(1 << 20) // math.isqrt(rank ** lean) + 1 for rank in range(1, count + 1)]
    largest = bound if full else min(bound, max(-(-total // count), total * weights[0] // sum(weights)))
    least = 1 if total - largest >= count - 1 else 0
    given, spare = [largest] + [least] * (count - 1), total - largest - least * (count - 1)
    while spare > 0:
        movable = [i for i in range(1, count) if given[i] < largest] or [i for i in range(1, count) if given[i] < bound]
        whole, remaining = sum([weights[i] for i in movable]), spare
        for i in movable:
            more = min(bound - given[i], max(1, remaining * weights[i] // whole), spare)
            given[i] = given[i] + more
            spare = spare - more
    return np.array(given)


def centred(key, extent, scale, reach, shards=(), kind=jnp.bfloat16):
    array = jax.random.normal(key, extent, jnp.float32) * scale
    if len(shards) > 0:
        array = levels(key, extent, shards, -0.22, 0.18) * array
    return jnp.clip(array, min=-reach, max=reach).astype(kind)


def setup_inputs(seed: int = 0, part: int = 0) -> dict:
    seeds = jax.random.split(jax.random.key(seed), 8)
    part_keys = jax.random.split(jax.random.fold_in(seeds[7], part), 8)
    point_traces = centred(part_keys[0], (ELEMS, 3, FACE, NT), 1.0, 6.0, ((0, 32),))
    rec_element = touch_ends(jax.random.randint(part_keys[1], (STATIONS,), 0, ELEM_DEV), jax.random.fold_in(part_keys[1], 1), 0, ELEM_DEV - 1).astype(jnp.int32)
    rec_coords = jnp.clip(jax.random.uniform(part_keys[2], (2, STATIONS), jnp.float32, -0.95, 0.95) * levels(part_keys[2], (2, STATIONS), ((1, 32),), -0.4, 0.0), -0.95, 0.95)
    slot_block_keys = jax.random.split(jax.random.fold_in(part_keys[3], 1), STATIONS // R_DEV)
    slot_block_turns = jax.random.permutation(jax.random.fold_in(part_keys[3], 3), STATIONS // R_DEV)
    slot_block = jax.vmap(lambda own, number: deal_out(jax.random.fold_in(part_keys[3], 2), own, number, R_DEV, N_CUTS, 1, CAP, 2))(slot_block_keys, slot_block_turns).reshape((STATIONS, 1))
    window_start = draw_window_start(jax.random.fold_in(jax.random.fold_in(seeds[7], part), 71), part)
    window_end = draw_window_end(jax.random.fold_in(jax.random.fold_in(seeds[7], part), 71), part)
    obs_windows = centred(part_keys[6], (N_CUTS * N_CUTS * CAP, 3, WIN), 1.0, 6.0, ((0, 32),))
    return dict(point_traces=point_traces, rec_element=rec_element, rec_coords=rec_coords, slot_block=slot_block, window_start=window_start, window_end=window_end, obs_windows=obs_windows)


gll_nodes = (-1.0, -0.6546536707079771, 0.0, 0.6546536707079771, 1.0)

def lagrange_basis(coordinate):
    columns = []
    for first_node in range(5):
        value = jnp.ones_like(coordinate)
        for other_node in range(5):
            if other_node != first_node:
                value = value * (coordinate - gll_nodes[other_node]) / (gll_nodes[first_node] - gll_nodes[other_node])
        columns.append(value)
    return jnp.stack(columns, axis=1)

def point_weights(rec_coords):
    along_xi = lagrange_basis(rec_coords[0])
    along_eta = lagrange_basis(rec_coords[1])
    return (along_xi[:, :, None] * along_eta[:, None, :]).reshape(rec_coords.shape[1], -1)

def make_table(window_len, freqs):
    sample = jnp.arange(window_len, dtype=jnp.int32)
    column = jnp.arange(freqs, dtype=jnp.int32)
    phase = sample[:, None] * column[None, :] % window_len
    angle = phase.astype(jnp.float32) * (2.0 * math.pi / window_len)
    return jnp.concatenate([jnp.cos(angle), jnp.sin(angle)], axis=1).astype(jnp.bfloat16)

def measure(synthetic, observed, lengths, weight_scale, spectrum_table):
    rows_here = synthetic.shape[0]
    window_len = synthetic.shape[2]
    freqs = spectrum_table.shape[1] // 2
    sample = jnp.arange(window_len, dtype=jnp.float32)
    orders = jnp.arange(1, TAPERS + 1, dtype=jnp.float32)
    span = lengths.astype(jnp.float32)
    inside = (sample[None, :] < span[:, None]).astype(jnp.float32)
    tapers = math.sqrt(2.0) * jnp.sin(math.pi * orders[None, :, None] * (sample[None, None, :] + 1.0) / (span[:, None, None] + 1.0)) * inside[:, None, :]
    observed_f = observed.astype(jnp.float32)
    energy = lax.optimization_barrier(jnp.sum(observed_f * observed_f * inside[:, None, :], axis=(1, 2))) / (3.0 * span) + 1e-05
    residual_wave = synthetic.astype(jnp.float32) - observed_f
    tapered = (tapers[:, :, None, :] * residual_wave[:, None, :, :]).astype(jnp.bfloat16)
    spectra = jnp.dot(tapered.reshape(-1, window_len), spectrum_table, preferred_element_type=jnp.float32)
    factor = weight_scale / (TAPERS * freqs * energy)
    misfit = 0.5 * jnp.sum(factor * lax.optimization_barrier(jnp.sum((spectra * spectra).reshape(rows_here, -1), axis=1)))
    rebuilt = lax.dot_general(spectra.astype(jnp.bfloat16), spectrum_table, (((1,), (1,)), ((), ())), preferred_element_type=jnp.float32)
    rebuilt = rebuilt.reshape(rows_here, TAPERS, 3, window_len)
    adjoint = (factor[:, None, None] * lax.optimization_barrier(jnp.sum(tapers[:, :, None, :] * rebuilt, axis=1))).astype(jnp.bfloat16)
    return (adjoint, misfit)

def reference(point_traces, rec_element, rec_coords, slot_block, window_start, window_end, obs_windows):
    stations = rec_element.shape[0]
    window_len = obs_windows.shape[2]
    face_points = point_traces.shape[2]
    capacity = obs_windows.shape[0] // (N_CUTS * N_CUTS)
    per_slice = stations // N_CUTS
    blocks = slot_block[:, 0]
    lengths = window_end - window_start
    weights = point_weights(rec_coords)
    source = jnp.arange(stations, dtype=jnp.int32) // per_slice
    elements = (rec_element + source * ELEM_DEV).astype(jnp.int32)
    starts = window_start.astype(jnp.int32)
    anchor = jnp.zeros((), jnp.int32)

    def pick(packed):
        element, offset, row_weights = packed
        element = element.astype(jnp.int32)
        offset = offset.astype(jnp.int32)
        window_piece = lax.dynamic_slice(point_traces, (element, anchor, anchor, offset), (1, 3, face_points, window_len))[0]
        return lax.optimization_barrier(jnp.sum(window_piece.astype(jnp.float32) * row_weights[None, :, None], axis=1))
    synthetic = lax.map(pick, (elements, starts, weights)).astype(jnp.bfloat16)
    grouped = blocks.reshape(N_CUTS, per_slice)
    same_block = grouped[:, :, None] == grouped[:, None, :]
    earlier = jnp.arange(per_slice)[None, :] < jnp.arange(per_slice)[:, None]
    slot_rank = lax.optimization_barrier(jnp.sum((same_block & earlier[None]).astype(jnp.int32), axis=2)).reshape(stations)
    obs_row = (blocks * (N_CUTS * capacity) + source * capacity + slot_rank).astype(jnp.int32)
    observed = obs_windows[obs_row]
    onehot = (blocks[:, None] == jnp.arange(N_CUTS, dtype=jnp.int32)[None, :]).astype(jnp.float32)
    counts = lax.optimization_barrier(jnp.sum(onehot, axis=0))
    weight_scale = per_slice / lax.optimization_barrier(jnp.sum(onehot * counts[None, :], axis=1))
    spectrum_table = make_table(window_len, NF)
    adjoint, misfit = measure(synthetic, observed, lengths, weight_scale, spectrum_table)
    total_misfit = jnp.reshape(misfit / (3.0 * window_len * stations), (1,))

    def spread(station, accumulated):
        station = jnp.asarray(station).astype(jnp.int32)
        element = elements[station].astype(jnp.int32)
        offset = starts[station].astype(jnp.int32)
        contribution = weights[station][None, :, None] * adjoint[station].astype(jnp.float32)[:, None, :]
        current = lax.dynamic_slice(accumulated, (element, anchor, anchor, offset), (1, 3, face_points, window_len))
        return lax.dynamic_update_slice(accumulated, current + contribution[None], (element, anchor, anchor, offset))
    accumulated = lax.fori_loop(0, stations, spread, jnp.zeros(point_traces.shape, jnp.float32))
    return (accumulated.astype(jnp.bfloat16), total_misfit)
```

```python
import math

import jax
import jax.numpy as jnp
from jax import lax
from jax.experimental import pallas as pl
from jax.experimental.pallas import tpu as pltpu
from jax.sharding import PartitionSpec as P

TAPERS = 5
NF = 512
COMPS = 3
LANES = 128
SUBLANES = 8
FACE = 25
FACE_PAD = 32
PIECE = 56
VMEM_LIMIT = 48 * 1024 * 1024

gll_nodes = (-1.0, -0.6546536707079771, 0.0, 0.6546536707079771, 1.0)


def lagrange_values(coordinate):
    values = []
    for first_node in range(5):
        value = jnp.ones_like(coordinate)
        for other_node in range(5):
            if other_node != first_node:
                value = (
                    value
                    * (coordinate - gll_nodes[other_node])
                    / (gll_nodes[first_node] - gll_nodes[other_node])
                )
        values.append(value)
    return values


def choose(index, values):
    chosen = jnp.where(index == 0, values[0], 0.0)
    for at in range(1, len(values)):
        chosen = jnp.where(index == at, values[at], chosen)
    return chosen


def third_part(weights, part):
    high = weights.astype(jnp.bfloat16).astype(jnp.float32)
    middle = (weights - high).astype(jnp.bfloat16).astype(jnp.float32)
    low = weights - high - middle
    kept = jnp.where(part == 0, high, jnp.where(part == 1, middle, jnp.where(part == 2, low, 0.0)))
    return kept.astype(jnp.bfloat16)


def iota(shape, dim):
    return lax.broadcasted_iota(jnp.int32, shape, dim)


def pack_kernel(block_ref, obs_ref, out_ref, rows):
    pairs = out_ref.shape[0]
    tiles = obs_ref.shape[2] // LANES
    for comp in range(COMPS):
        for tile in range(tiles):
            values = obs_ref[comp, :, tile * LANES : (tile + 1) * LANES].astype(jnp.float32)
            rows[comp, pl.ds(tile, 2 * pairs, stride=tiles), :] = values
    names = block_ref[...]
    square = (pairs, names.shape[1])
    own = jnp.where(iota(square, 0) == iota(square, 1), jnp.broadcast_to(names, square), 0)
    column = jnp.sum(own, axis=1, keepdims=True)
    hits = jnp.where(iota((pairs, LANES), 1) == column, 1.0, 0.0)
    histogram = jnp.sum(hits, axis=0, keepdims=True)
    tail = jnp.where(iota((SUBLANES, LANES), 0) == 0, histogram, 0.0).astype(jnp.bfloat16)
    for pair in range(pairs):
        for comp in range(COMPS):
            out_ref[pair, 16 * comp : 16 * comp + 16, :] = rows[comp, 16 * pair : 16 * pair + 16, :].astype(jnp.bfloat16)
        out_ref[pair, 48:56, :] = tail


def synth_kernel(
    start_ref, columns_ref, rows_ref, traces_ref, syn_ref, taper_ref, square_ref, spread_ref, wide, moved
):
    elements = traces_ref.shape[0]
    stations = columns_ref.shape[0]
    window = syn_ref.shape[2]
    tiles = window // LANES
    all_tiles = traces_ref.shape[3] // LANES
    step = SUBLANES * stations

    columns = columns_ref[...]
    element = columns[:, 2:3]
    span = columns[:, 3:4]

    face = iota((stations, FACE_PAD), 1)
    along_xi = choose(face // 5, lagrange_values(columns[:, 0:1]))
    along_eta = choose(face % 5, lagrange_values(columns[:, 1:2]))
    weights = jnp.where(face < FACE, along_xi * along_eta, 0.0)
    by_station = [third_part(weights, part).astype(jnp.float32) for part in range(3)]
    by_station = jnp.concatenate(by_station, axis=0)
    elements_3 = jnp.concatenate([element, element, element], axis=0)

    for comp in range(COMPS):
        total = None
        for at in range(elements):
            here = jnp.where(elements_3 == at, by_station, 0.0).astype(jnp.bfloat16)[:, :FACE]
            term = jnp.dot(here, traces_ref[at, comp], preferred_element_type=jnp.float32)
            total = term if total is None else total + term
        sampled = total[:stations] + total[stations : 2 * stations] + total[2 * stations : 3 * stations]
        for tile in range(all_tiles):
            wide[pl.ds(tile * step + comp, stations, stride=SUBLANES), :] = sampled[
                :, tile * LANES : (tile + 1) * LANES
            ]
    wide[all_tiles * step :, :] = jnp.zeros((step, LANES), jnp.float32)

    lane = iota((SUBLANES, LANES), 1)

    def cut(station, carry):
        start = start_ref[station]
        first = start // LANES
        shift = start % LANES
        back = (LANES - shift) % LANES
        keep = lane < LANES - shift
        turned = []
        for tile in range(tiles + 1):
            at = pl.multiple_of((first + tile) * step + station * SUBLANES, SUBLANES)
            turned.append(pltpu.roll(wide[pl.ds(at, SUBLANES), :], back, 1))
        for tile in range(tiles):
            at = pl.multiple_of(tile * step + station * SUBLANES, SUBLANES)
            moved[pl.ds(at, SUBLANES), :] = jnp.where(keep, turned[tile], turned[tile + 1])
        return carry

    lax.fori_loop(0, stations, cut, 0)

    for comp in range(COMPS):
        for tile in range(tiles):
            piece = moved[pl.ds(tile * step + comp, stations, stride=SUBLANES), :]
            syn_ref[comp, :, tile * LANES : (tile + 1) * LANES] = piece.astype(jnp.bfloat16).astype(jnp.float32)

    for tile in range(tiles):
        lanes = slice(tile * LANES, (tile + 1) * LANES)
        sample = iota((stations, LANES), 1).astype(jnp.float32) + float(tile * LANES)
        inside = sample < span
        angle = jnp.where(inside, math.pi * (sample + 1.0) / (span + 1.0), 0.0)
        first = math.sqrt(2.0) * jnp.sin(angle)
        twice = 2.0 * jnp.cos(angle)
        tapers = [jnp.where(inside, first, 0.0)]
        tapers.append(twice * tapers[0])
        for _ in range(2, TAPERS):
            tapers.append(twice * tapers[-1] - tapers[-2])
        squares = tapers[0] * tapers[0]
        taper_ref[0, :, lanes] = tapers[0]
        for order in range(1, TAPERS):
            taper_ref[order, :, lanes] = tapers[order]
            squares = squares + tapers[order] * tapers[order]
        square_ref[:, lanes] = float(NF) * squares

    rows = rows_ref[...]
    height = elements * FACE_PAD
    place = iota((height, LANES), 0)
    face = place % FACE_PAD
    along_xi = choose(face // 5, lagrange_values(rows[0:1, :]))
    along_eta = choose(face % 5, lagrange_values(rows[1:2, :]))
    mine = (face < FACE) & ((place // FACE_PAD).astype(jnp.float32) == rows[2:3, :])
    weights = jnp.where(mine, along_xi * along_eta, 0.0)
    spread_ref[...] = third_part(weights, iota((height, LANES), 1) // stations)


def misfit_kernel(
    block_ref, rank_ref, columns_ref, taken_ref, syn_ref, taper_ref, square_ref,
    partial_ref, residual_ref, other_ref, factor_ref, picked, sums,
):
    stations = columns_ref.shape[0]
    pairs = taken_ref.shape[0]
    window = syn_ref.shape[2]
    tiles = window // LANES
    columns = columns_ref[...]
    for station in range(stations):
        block = block_ref[station]
        second = rank_ref[station] > 0
        for comp in range(COMPS):
            both = taken_ref[block, 16 * comp : 16 * comp + 16, :].astype(jnp.float32)
            at = (comp * stations + station) * tiles
            picked[at : at + tiles, :] = jnp.where(second, both[tiles:], both[:tiles])

    counts = taken_ref[0, 48:56, :].astype(jnp.float32)
    for pair in range(1, pairs):
        counts = counts + taken_ref[pair, 48:56, :].astype(jnp.float32)
    name = columns[:, 4:5]
    lane_f = iota((stations, LANES), 1).astype(jnp.float32)
    count = jnp.sum(jnp.where(lane_f == name, counts[0:1, :], 0.0), axis=1, keepdims=True)

    lane = iota((SUBLANES, LANES), 1).astype(jnp.float32)
    energies, powers = [], []
    for group in range(stations // SUBLANES):
        rows = slice(group * SUBLANES, (group + 1) * SUBLANES)
        span = columns[rows, 3:4]
        energy = jnp.zeros((SUBLANES, LANES), jnp.float32)
        power = jnp.zeros((SUBLANES, LANES), jnp.float32)
        parts = [jnp.zeros((SUBLANES, LANES), jnp.float32) for _ in range(TAPERS * COMPS)]
        for tile in range(tiles):
            lanes = slice(tile * LANES, (tile + 1) * LANES)
            inside = lane + float(tile * LANES) < span
            observed, residual = [], []
            for comp in range(COMPS):
                at = (comp * stations + group * SUBLANES) * tiles + tile
                observed.append(picked[pl.ds(at, SUBLANES, stride=tiles), :])
                residual.append(syn_ref[comp, rows, lanes] - observed[comp])
                residual_ref[comp, rows, lanes] = residual[comp]
            squares = observed[0] * observed[0] + observed[1] * observed[1] + observed[2] * observed[2]
            energy = energy + jnp.where(inside, squares, 0.0)
            squares = residual[0] * residual[0] + residual[1] * residual[1] + residual[2] * residual[2]
            power = power + square_ref[rows, lanes] * squares
            for order in range(TAPERS):
                taper = taper_ref[order, rows, lanes]
                for comp in range(COMPS):
                    at = order * COMPS + comp
                    parts[at] = parts[at] + taper * residual[comp]
        for at in range(TAPERS * COMPS):
            start = at * stations + group * SUBLANES
            sums[start : start + SUBLANES, :] = parts[at]
        energies.append(energy)
        powers.append(power)

    odd = (iota((LANES, LANES), 0) + iota((LANES, LANES), 1)) % 2
    odd = odd.astype(jnp.float32).astype(jnp.bfloat16)
    whole = sums[...]
    high = whole.astype(jnp.bfloat16)
    low = (whole - high.astype(jnp.float32)).astype(jnp.bfloat16)
    other = jnp.dot(high, odd, preferred_element_type=jnp.float32) + jnp.dot(
        low, odd, preferred_element_type=jnp.float32
    )
    other_ref[...] = other
    product = whole * other
    power = jnp.concatenate(powers, axis=0)
    for at in range(TAPERS * COMPS):
        power = power + product[at * stations : (at + 1) * stations]
    energy = jnp.sum(jnp.concatenate(energies, axis=0), axis=1, keepdims=True)
    power = jnp.sum(power, axis=1, keepdims=True)
    energy = energy / (3.0 * columns[:, 3:4]) + 1e-05
    weight = float(stations) / count
    factor = weight / (float(TAPERS * NF) * energy)
    factor_ref[...] = jnp.broadcast_to(factor, factor_ref.shape)
    partial = jnp.sum(0.5 * (factor * power), axis=0, keepdims=True)
    partial_ref[...] = jnp.broadcast_to(partial[:, :, None], partial_ref.shape)


def spread_kernel(
    start_ref, residual_ref, taper_ref, square_ref, other_ref, factor_ref, spread_ref, out_ref, source, placed
):
    elements = out_ref.shape[0]
    stations = factor_ref.shape[0]
    tiles = residual_ref.shape[2] // LANES
    all_tiles = out_ref.shape[3] // LANES
    step = SUBLANES * stations
    for comp in range(COMPS):
        for group in range(stations // SUBLANES):
            rows = slice(group * SUBLANES, (group + 1) * SUBLANES)
            factor = factor_ref[rows, :]
            for tile in range(tiles):
                lanes = slice(tile * LANES, (tile + 1) * LANES)
                value = square_ref[rows, lanes] * residual_ref[comp, rows, lanes]
                for order in range(TAPERS):
                    at = (order * COMPS + comp) * stations + group * SUBLANES
                    value = value + taper_ref[order, rows, lanes] * other_ref[at : at + SUBLANES, :]
                value = (factor * value).astype(jnp.bfloat16).astype(jnp.float32)
                at = tile * step + group * SUBLANES * SUBLANES + comp
                source[pl.ds(at, SUBLANES, stride=SUBLANES), :] = value

    placed[...] = jnp.zeros(placed.shape, jnp.float32)
    lane = iota((SUBLANES, LANES), 1)

    def put(station, carry):
        start = start_ref[station]
        first = start // LANES
        shift = start % LANES
        keep = lane >= shift
        turned = [jnp.zeros((SUBLANES, LANES), jnp.float32)]
        for tile in range(tiles):
            at = pl.multiple_of(tile * step + station * SUBLANES, SUBLANES)
            turned.append(pltpu.roll(source[pl.ds(at, SUBLANES), :], shift, 1))
        turned.append(turned[0])
        for tile in range(tiles + 1):
            at = pl.multiple_of((first + tile) * step + station * SUBLANES, SUBLANES)
            placed[pl.ds(at, SUBLANES), :] = jnp.where(keep, turned[tile + 1], turned[tile])
        return carry

    lax.fori_loop(0, stations, put, 0)

    weights = spread_ref[:, : 3 * stations]
    for comp in range(COMPS):
        pieces = []
        for tile in range(all_tiles):
            piece = placed[pl.ds(tile * step + comp, stations, stride=SUBLANES), :]
            pieces.append(piece.astype(jnp.bfloat16))
        values = jnp.concatenate(pieces, axis=1)
        values = jnp.concatenate([values, values, values], axis=0)
        result = jnp.dot(weights, values, preferred_element_type=jnp.float32)
        for at in range(elements):
            rows = slice(at * FACE_PAD, at * FACE_PAD + FACE)
            out_ref[at, comp, :, :] = result[rows].astype(out_ref.dtype)


def whole(space=pltpu.VMEM):
    return pl.BlockSpec(memory_space=space)


def local(point_traces, rec_element, rec_coords, slot_block, window_start, window_end, obs_windows):
    slices = lax.axis_size("cuts")
    stations = rec_element.shape[0]
    window = obs_windows.shape[2]
    tiles = window // LANES
    samples = point_traces.shape[3]
    elements = point_traces.shape[0]
    blocks = slot_block[:, 0]
    params = pltpu.CompilerParams(vmem_limit_bytes=VMEM_LIMIT)
    f32 = jnp.float32

    packed = pl.pallas_call(
        pack_kernel,
        out_shape=jax.ShapeDtypeStruct((slices, PIECE, LANES), jnp.bfloat16),
        in_specs=[whole(), whole()],
        out_specs=whole(),
        scratch_shapes=[pltpu.VMEM((COMPS, obs_windows.shape[0] * tiles, LANES), f32)],
        compiler_params=params,
        cost_estimate=pl.CostEstimate(flops=0, bytes_accessed=1 << 20, transcendentals=0),
        name="pack_observed",
    )(blocks.reshape(1, stations), jnp.transpose(obs_windows, (1, 0, 2)))
    taken = lax.all_to_all(packed, "cuts", split_axis=0, concat_axis=0, tiled=True)

    same_block = blocks[:, None] == blocks[None, :]
    earlier = jnp.arange(stations)[None, :] < jnp.arange(stations)[:, None]
    slot_rank = jnp.sum((same_block & earlier).astype(jnp.int32), axis=1)
    lengths = (window_end - window_start).astype(f32)
    rows = jnp.stack(
        [rec_coords[0], rec_coords[1], rec_element.astype(f32), lengths, blocks.astype(f32)]
        + [jnp.zeros((stations,), f32)] * 3
    )
    columns = rows.T
    rows = jnp.tile(rows, (1, LANES // stations))

    step = SUBLANES * stations
    synthetic, tapers, squares, spread_weights = pl.pallas_call(
        synth_kernel,
        out_shape=(
            jax.ShapeDtypeStruct((COMPS, stations, window), f32),
            jax.ShapeDtypeStruct((TAPERS, stations, window), f32),
            jax.ShapeDtypeStruct((stations, window), f32),
            jax.ShapeDtypeStruct((elements * FACE_PAD, LANES), jnp.bfloat16),
        ),
        in_specs=[whole(pltpu.SMEM)] + [whole()] * 3,
        out_specs=(whole(),) * 4,
        scratch_shapes=[
            pltpu.VMEM(((samples // LANES + 1) * step, LANES), f32),
            pltpu.VMEM((tiles * step, LANES), f32),
        ],
        compiler_params=params,
        cost_estimate=pl.CostEstimate(
            flops=2 * 96 * 32 * 18 * samples, bytes_accessed=4 << 20, transcendentals=2 * stations * window
        ),
        name="synthetics",
    )(window_start, columns, rows, point_traces)

    partial, residual, other, factor = pl.pallas_call(
        misfit_kernel,
        out_shape=(
            jax.ShapeDtypeStruct((slices, 1, LANES), f32),
            jax.ShapeDtypeStruct((COMPS, stations, window), f32),
            jax.ShapeDtypeStruct((TAPERS * COMPS * stations, LANES), f32),
            jax.ShapeDtypeStruct((stations, LANES), f32),
        ),
        in_specs=[whole(pltpu.SMEM)] * 2 + [whole()] * 5,
        out_specs=(whole(),) * 4,
        scratch_shapes=[
            pltpu.VMEM((COMPS * stations * tiles, LANES), f32),
            pltpu.VMEM((TAPERS * COMPS * stations, LANES), f32),
        ],
        compiler_params=params,
        cost_estimate=pl.CostEstimate(flops=1 << 24, bytes_accessed=3 << 20, transcendentals=0),
        name="misfit",
    )(blocks, slot_rank, columns, taken, synthetic, tapers, squares)
    partials = lax.all_to_all(partial, "cuts", split_axis=0, concat_axis=0, tiled=True)

    adjoint_points = pl.pallas_call(
        spread_kernel,
        out_shape=jax.ShapeDtypeStruct(point_traces.shape, point_traces.dtype),
        in_specs=[whole(pltpu.SMEM)] + [whole()] * 6,
        out_specs=whole(),
        scratch_shapes=[
            pltpu.VMEM((tiles * step, LANES), f32),
            pltpu.VMEM(((samples // LANES + 1) * step, LANES), f32),
        ],
        compiler_params=params,
        cost_estimate=pl.CostEstimate(
            flops=2 * 192 * 96 * 3 * samples, bytes_accessed=6 << 20, transcendentals=0
        ),
        name="spread_adjoint",
    )(window_start, residual, tapers, squares, other, factor, spread_weights)

    total = jnp.sum(partials[:, 0, 0])
    total_misfit = jnp.reshape(total / (3.0 * window * stations * slices), (1,))
    return (adjoint_points, total_misfit)


def solution(mesh):
    return jax.shard_map(
        local,
        mesh=mesh,
        in_specs=(
            P(("event", "cuts"), None, None, None),
            P(("event", "cuts")),
            P(None, ("event", "cuts")),
            P(("event", "cuts"), None),
            P(("event", "cuts")),
            P(("event", "cuts")),
            P(("event", "cuts"), None, None),
        ),
        out_specs=(P(("event", "cuts"), None, None, None), P("event")),
        check_vma=False,
    )
```

```python
import math

import jax
import jax.numpy as jnp
from jax import lax
from jax.experimental import pallas as pl
from jax.experimental.pallas import tpu as pltpu
from jax.sharding import PartitionSpec as P

TAPERS = 5
NF = 512
COMPS = 3
LANES = 128
SUBLANES = 8
FACE = 25
FACE_PAD = 32
PIECE = 56
VMEM_LIMIT = 48 * 1024 * 1024
UNROLL = 8

gll_nodes = (-1.0, -0.6546536707079771, 0.0, 0.6546536707079771, 1.0)


def lagrange_values(coordinate):
    values = []
    for first_node in range(5):
        value = jnp.ones_like(coordinate)
        for other_node in range(5):
            if other_node != first_node:
                value = (
                    value
                    * (coordinate - gll_nodes[other_node])
                    / (gll_nodes[first_node] - gll_nodes[other_node])
                )
        values.append(value)
    return values


def choose(index, values):
    chosen = jnp.where(index == 0, values[0], 0.0)
    for at in range(1, len(values)):
        chosen = jnp.where(index == at, values[at], chosen)
    return chosen


def third_part(weights, part):
    high = weights.astype(jnp.bfloat16).astype(jnp.float32)
    middle = (weights - high).astype(jnp.bfloat16).astype(jnp.float32)
    low = weights - high - middle
    kept = jnp.where(part == 0, high, jnp.where(part == 1, middle, jnp.where(part == 2, low, 0.0)))
    return kept.astype(jnp.bfloat16)


def iota(shape, dim):
    return lax.broadcasted_iota(jnp.int32, shape, dim)


def pack_kernel(block_ref, obs_ref, out_ref, raw, names_vmem, rows, sems):
    pairs = out_ref.shape[0]
    tiles = obs_ref.shape[2] // LANES
    fetches = [pltpu.make_async_copy(obs_ref.at[comp], raw.at[comp], sems.at[comp]) for comp in range(COMPS)]
    fetches.append(pltpu.make_async_copy(block_ref, names_vmem, sems.at[COMPS]))
    for fetch in fetches:
        fetch.start()
    for comp in range(COMPS):
        fetches[comp].wait()
        for tile in range(tiles):
            values = raw[comp, :, tile * LANES : (tile + 1) * LANES].astype(jnp.float32)
            rows[comp, pl.ds(tile, 2 * pairs, stride=tiles), :] = values
        for pair in range(pairs):
            piece = rows[comp, 16 * pair : 16 * pair + 16, :].astype(jnp.bfloat16)
            out_ref[pair, 16 * comp : 16 * comp + 16, :] = piece
    fetches[COMPS].wait()
    column = as_column(names_vmem[...].astype(jnp.float32))
    hits = jnp.where(iota((pairs, LANES), 1).astype(jnp.float32) == column, 1.0, 0.0)
    histogram = jnp.sum(hits, axis=0, keepdims=True)
    tail = jnp.where(iota((SUBLANES, LANES), 0) == 0, histogram, 0.0).astype(jnp.bfloat16)
    for pair in range(pairs):
        out_ref[pair, 48:56, :] = tail


def as_column(row):
    square = (row.shape[1], row.shape[1])
    own = jnp.where(iota(square, 0) == iota(square, 1), jnp.broadcast_to(row, square), 0.0)
    return jnp.sum(own, axis=1, keepdims=True)


def as_row(column):
    tall = (column.shape[0], LANES)
    own = jnp.where(iota(tall, 0) == iota(tall, 1) % column.shape[0], jnp.broadcast_to(column, tall), 0.0)
    return jnp.sum(own, axis=0, keepdims=True)


def synth_kernel(
    element_ref, coords_ref, block_ref, start_ref, end_ref, traces_ref,
    syn_ref, taper_ref, square_ref, spread_ref, columns_ref,
    element_vmem, coords_vmem, block_vmem, start_vmem, end_vmem, start_smem, traces, wide, moved, sems,
):
    elements = traces_ref.shape[0]
    stations = syn_ref.shape[1]
    window = syn_ref.shape[2]
    tiles = window // LANES
    all_tiles = traces_ref.shape[3] // LANES
    step = SUBLANES * stations
    pairs = [
        (element_ref, element_vmem), (coords_ref, coords_vmem), (block_ref, block_vmem),
        (start_ref, start_vmem), (end_ref, end_vmem), (start_ref, start_smem),
    ]
    small = [pltpu.make_async_copy(a, b, sems.at[at]) for at, (a, b) in enumerate(pairs)]
    large = [
        pltpu.make_async_copy(traces_ref.at[:, comp], traces.at[comp], sems.at[len(pairs) + comp])
        for comp in range(COMPS)
    ]
    for fetch in small + large:
        fetch.start()
    for fetch in small:
        fetch.wait()

    span_row = (end_vmem[...] - start_vmem[...]).astype(jnp.float32)
    name_row = block_vmem[...].astype(jnp.float32)
    xi = as_column(coords_vmem[0:1, :])
    eta = as_column(coords_vmem[1:2, :])
    element = as_column(element_vmem[...].astype(jnp.float32))
    span = as_column(span_row)
    name = as_column(name_row)
    square = (stations, stations)
    twin = (jnp.broadcast_to(name_row, square) == name) & (iota(square, 1) < iota(square, 0))
    rank = jnp.sum(jnp.where(twin, 1.0, 0.0), axis=1, keepdims=True)
    columns_ref[...] = choose(iota((stations, LANES), 1), [span, name, rank])

    for tile in range(tiles):
        lanes = slice(tile * LANES, (tile + 1) * LANES)
        sample = iota((stations, LANES), 1).astype(jnp.float32) + float(tile * LANES)
        inside = sample < span
        angle = jnp.where(inside, math.pi * (sample + 1.0) / (span + 1.0), 0.0)
        first = math.sqrt(2.0) * jnp.sin(angle)
        twice = 2.0 * jnp.cos(angle)
        tapers = [jnp.where(inside, first, 0.0)]
        tapers.append(twice * tapers[0])
        for _ in range(2, TAPERS):
            tapers.append(twice * tapers[-1] - tapers[-2])
        squares = tapers[0] * tapers[0]
        taper_ref[0, :, lanes] = tapers[0]
        for order in range(1, TAPERS):
            taper_ref[order, :, lanes] = tapers[order]
            squares = squares + tapers[order] * tapers[order]
        square_ref[:, lanes] = float(NF) * squares

    height = elements * FACE_PAD
    face = iota((FACE_PAD, LANES), 0)
    along_xi = choose(face // 5, lagrange_values(as_row(xi)))
    along_eta = choose(face % 5, lagrange_values(as_row(eta)))
    weights = jnp.where(face < FACE, along_xi * along_eta, 0.0)
    thirds = third_part(weights, iota((FACE_PAD, LANES), 1) // stations).astype(jnp.float32)
    element_row = as_row(element)
    for at in range(elements):
        spread_ref[at * FACE_PAD : (at + 1) * FACE_PAD, :] = jnp.where(element_row == at, thirds, 0.0).astype(jnp.bfloat16)

    face = iota((stations, FACE_PAD), 1)
    along_xi = choose(face // 5, lagrange_values(xi))
    along_eta = choose(face % 5, lagrange_values(eta))
    weights = jnp.where(face < FACE, along_xi * along_eta, 0.0)
    by_station = [third_part(weights, part).astype(jnp.float32) for part in range(3)]
    by_station = jnp.concatenate(by_station, axis=0)
    elements_3 = jnp.concatenate([element, element, element], axis=0)
    here = [jnp.where(elements_3 == at, by_station, 0.0).astype(jnp.bfloat16)[:, :FACE] for at in range(elements)]

    for comp in range(COMPS):
        large[comp].wait()
        total = None
        for at in range(elements):
            term = jnp.dot(here[at], traces[comp, at], preferred_element_type=jnp.float32)
            total = term if total is None else total + term
        sampled = total[:stations] + total[stations : 2 * stations] + total[2 * stations : 3 * stations]
        for tile in range(all_tiles):
            wide[pl.ds(tile * step + comp, stations, stride=SUBLANES), :] = sampled[
                :, tile * LANES : (tile + 1) * LANES
            ]
    wide[all_tiles * step :, :] = jnp.zeros((step, LANES), jnp.float32)

    lane = iota((SUBLANES, LANES), 1)

    def cut(station, carry):
        start = start_smem[0, station]
        first = start // LANES
        shift = start % LANES
        back = (LANES - shift) % LANES
        keep = lane < LANES - shift
        turned = []
        for tile in range(tiles + 1):
            at = pl.multiple_of((first + tile) * step + station * SUBLANES, SUBLANES)
            turned.append(pltpu.roll(wide[pl.ds(at, SUBLANES), :], back, 1))
        for tile in range(tiles):
            at = pl.multiple_of(tile * step + station * SUBLANES, SUBLANES)
            moved[pl.ds(at, SUBLANES), :] = jnp.where(keep, turned[tile], turned[tile + 1])
        return carry

    lax.fori_loop(0, stations, cut, 0, unroll=UNROLL)

    for comp in range(COMPS):
        for tile in range(tiles):
            piece = moved[pl.ds(tile * step + comp, stations, stride=SUBLANES), :]
            syn_ref[comp, :, tile * LANES : (tile + 1) * LANES] = piece.astype(jnp.bfloat16).astype(jnp.float32)


def misfit_kernel(
    block_ref, columns_ref, taken_ref, syn_ref, taper_ref, square_ref,
    partial_ref, residual_ref, other_ref, factor_ref, block_smem, picked, sums, sem,
):
    stations = columns_ref.shape[0]
    pairs = taken_ref.shape[0]
    window = syn_ref.shape[2]
    tiles = window // LANES
    fetch = pltpu.make_async_copy(block_ref, block_smem, sem)
    fetch.start()
    columns = columns_ref[...]
    counts = taken_ref[0, 48:56, :].astype(jnp.float32)
    for pair in range(1, pairs):
        counts = counts + taken_ref[pair, 48:56, :].astype(jnp.float32)
    fetch.wait()
    for station in range(stations):
        block = block_smem[0, station]
        for comp in range(COMPS):
            at = (comp * stations + station) * 2 * tiles
            picked[at : at + 2 * tiles, :] = taken_ref[block, 16 * comp : 16 * comp + 16, :].astype(jnp.float32)
    name = columns[:, 1:2]
    lane_f = iota((stations, LANES), 1).astype(jnp.float32)
    count = jnp.sum(jnp.where(lane_f == name, counts[0:1, :], 0.0), axis=1, keepdims=True)

    lane = iota((SUBLANES, LANES), 1).astype(jnp.float32)
    energies, powers = [], []
    for group in range(stations // SUBLANES):
        rows = slice(group * SUBLANES, (group + 1) * SUBLANES)
        span = columns[rows, 0:1]
        second = columns[rows, 2:3] > 0.0
        energy = jnp.zeros((SUBLANES, LANES), jnp.float32)
        power = jnp.zeros((SUBLANES, LANES), jnp.float32)
        parts = [jnp.zeros((SUBLANES, LANES), jnp.float32) for _ in range(TAPERS * COMPS)]
        for tile in range(tiles):
            lanes = slice(tile * LANES, (tile + 1) * LANES)
            inside = lane + float(tile * LANES) < span
            observed, residual = [], []
            for comp in range(COMPS):
                at = (comp * stations + group * SUBLANES) * 2 * tiles + tile
                first_rank = picked[pl.ds(at, SUBLANES, stride=2 * tiles), :]
                second_rank = picked[pl.ds(at + tiles, SUBLANES, stride=2 * tiles), :]
                observed.append(jnp.where(second, second_rank, first_rank))
                residual.append(syn_ref[comp, rows, lanes] - observed[comp])
                residual_ref[comp, rows, lanes] = residual[comp]
            squares = observed[0] * observed[0] + observed[1] * observed[1] + observed[2] * observed[2]
            energy = energy + jnp.where(inside, squares, 0.0)
            squares = residual[0] * residual[0] + residual[1] * residual[1] + residual[2] * residual[2]
            power = power + square_ref[rows, lanes] * squares
            for order in range(TAPERS):
                taper = taper_ref[order, rows, lanes]
                for comp in range(COMPS):
                    at = order * COMPS + comp
                    parts[at] = parts[at] + taper * residual[comp]
        for at in range(TAPERS * COMPS):
            start = at * stations + group * SUBLANES
            sums[start : start + SUBLANES, :] = parts[at]
        energies.append(energy)
        powers.append(power)

    odd = (iota((LANES, LANES), 0) + iota((LANES, LANES), 1)) % 2
    odd = odd.astype(jnp.float32).astype(jnp.bfloat16)
    whole = sums[...]
    high = whole.astype(jnp.bfloat16)
    low = (whole - high.astype(jnp.float32)).astype(jnp.bfloat16)
    other = jnp.dot(high, odd, preferred_element_type=jnp.float32) + jnp.dot(
        low, odd, preferred_element_type=jnp.float32
    )
    other_ref[...] = other
    product = whole * other
    power = jnp.concatenate(powers, axis=0)
    for at in range(TAPERS * COMPS):
        power = power + product[at * stations : (at + 1) * stations]
    energy = jnp.sum(jnp.concatenate(energies, axis=0), axis=1, keepdims=True)
    power = jnp.sum(power, axis=1, keepdims=True)
    energy = energy / (3.0 * columns[:, 0:1]) + 1e-05
    weight = float(stations) / count
    factor = weight / (float(TAPERS * NF) * energy)
    factor_ref[...] = jnp.broadcast_to(factor, factor_ref.shape)
    partial = jnp.sum(0.5 * (factor * power), axis=0, keepdims=True)
    partial_ref[...] = jnp.broadcast_to(partial[:, :, None], partial_ref.shape)


def spread_kernel(
    start_ref, residual_ref, taper_ref, square_ref, other_ref, factor_ref, spread_ref,
    out_ref, start_smem, source, placed, staged, sems,
):
    fetch = pltpu.make_async_copy(start_ref, start_smem, sems.at[COMPS])
    fetch.start()
    elements = out_ref.shape[0]
    stations = factor_ref.shape[0]
    tiles = residual_ref.shape[2] // LANES
    all_tiles = out_ref.shape[3] // LANES
    step = SUBLANES * stations
    for comp in range(COMPS):
        for group in range(stations // SUBLANES):
            rows = slice(group * SUBLANES, (group + 1) * SUBLANES)
            factor = factor_ref[rows, :]
            for tile in range(tiles):
                lanes = slice(tile * LANES, (tile + 1) * LANES)
                value = square_ref[rows, lanes] * residual_ref[comp, rows, lanes]
                for order in range(TAPERS):
                    at = (order * COMPS + comp) * stations + group * SUBLANES
                    value = value + taper_ref[order, rows, lanes] * other_ref[at : at + SUBLANES, :]
                value = (factor * value).astype(jnp.bfloat16).astype(jnp.float32)
                at = tile * step + group * SUBLANES * SUBLANES + comp
                source[pl.ds(at, SUBLANES, stride=SUBLANES), :] = value

    placed[...] = jnp.zeros(placed.shape, jnp.float32)
    lane = iota((SUBLANES, LANES), 1)

    fetch.wait()

    def put(station, carry):
        start = start_smem[0, station]
        first = start // LANES
        shift = start % LANES
        keep = lane >= shift
        turned = [jnp.zeros((SUBLANES, LANES), jnp.float32)]
        for tile in range(tiles):
            at = pl.multiple_of(tile * step + station * SUBLANES, SUBLANES)
            turned.append(pltpu.roll(source[pl.ds(at, SUBLANES), :], shift, 1))
        turned.append(turned[0])
        for tile in range(tiles + 1):
            at = pl.multiple_of((first + tile) * step + station * SUBLANES, SUBLANES)
            placed[pl.ds(at, SUBLANES), :] = jnp.where(keep, turned[tile + 1], turned[tile])
        return carry

    lax.fori_loop(0, stations, put, 0, unroll=UNROLL)

    weights = spread_ref[:, : 3 * stations]
    for comp in range(COMPS):
        pieces = []
        for tile in range(all_tiles):
            piece = placed[pl.ds(tile * step + comp, stations, stride=SUBLANES), :]
            pieces.append(piece.astype(jnp.bfloat16))
        values = jnp.concatenate(pieces, axis=1)
        values = jnp.concatenate([values, values, values], axis=0)
        result = jnp.dot(weights, values, preferred_element_type=jnp.float32)
        for at in range(elements):
            rows = slice(at * FACE_PAD, at * FACE_PAD + FACE)
            staged[comp, at, :, :] = result[rows].astype(staged.dtype)
        pltpu.make_async_copy(staged.at[comp], out_ref.at[:, comp], sems.at[comp]).start()
    for comp in range(COMPS):
        pltpu.make_async_copy(staged.at[comp], out_ref.at[:, comp], sems.at[comp]).wait()


def whole(space=pltpu.VMEM):
    return pl.BlockSpec(memory_space=space)


def in_hbm(array):
    return pltpu.with_memory_space_constraint(array, pltpu.HBM)


def local(point_traces, rec_element, rec_coords, slot_block, window_start, window_end, obs_windows):
    slices = lax.axis_size("cuts")
    stations = rec_element.shape[0]
    window = obs_windows.shape[2]
    tiles = window // LANES
    samples = point_traces.shape[3]
    elements = point_traces.shape[0]
    line = (1, stations)
    blocks = in_hbm(slot_block.reshape(line))
    starts = in_hbm(window_start.reshape(line))
    params = pltpu.CompilerParams(vmem_limit_bytes=VMEM_LIMIT)
    f32, i32, bf16 = jnp.float32, jnp.int32, jnp.bfloat16
    far = whole(pltpu.HBM)

    packed = pl.pallas_call(
        pack_kernel,
        out_shape=pltpu.VMEM((slices, PIECE, LANES), bf16),
        in_specs=[far, far],
        out_specs=whole(),
        scratch_shapes=[
            pltpu.VMEM((COMPS, obs_windows.shape[0], window), bf16),
            pltpu.VMEM(line, i32),
            pltpu.VMEM((COMPS, obs_windows.shape[0] * tiles, LANES), f32),
            pltpu.SemaphoreType.DMA((COMPS + 1,)),
        ],
        compiler_params=params,
        cost_estimate=pl.CostEstimate(flops=0, bytes_accessed=1 << 20, transcendentals=0),
        name="pack_observed",
    )(blocks, in_hbm(jnp.transpose(obs_windows, (1, 0, 2))))
    taken = lax.all_to_all(packed, "cuts", split_axis=0, concat_axis=0, tiled=True)

    step = SUBLANES * stations
    synthetic, tapers, squares, spread_weights, columns = pl.pallas_call(
        synth_kernel,
        out_shape=(
            jax.ShapeDtypeStruct((COMPS, stations, window), f32),
            jax.ShapeDtypeStruct((TAPERS, stations, window), f32),
            jax.ShapeDtypeStruct((stations, window), f32),
            jax.ShapeDtypeStruct((elements * FACE_PAD, LANES), bf16),
            jax.ShapeDtypeStruct((stations, LANES), f32),
        ),
        in_specs=[far] * 6,
        out_specs=(whole(),) * 5,
        scratch_shapes=[
            pltpu.VMEM(line, i32),
            pltpu.VMEM((2, stations), f32),
            pltpu.VMEM(line, i32),
            pltpu.VMEM(line, i32),
            pltpu.VMEM(line, i32),
            pltpu.SMEM(line, i32),
            pltpu.VMEM((COMPS, elements) + point_traces.shape[2:], bf16),
            pltpu.VMEM(((samples // LANES + 1) * step, LANES), f32),
            pltpu.VMEM((tiles * step, LANES), f32),
            pltpu.SemaphoreType.DMA((6 + COMPS,)),
        ],
        compiler_params=params,
        cost_estimate=pl.CostEstimate(
            flops=2 * 96 * 32 * 18 * samples, bytes_accessed=4 << 20, transcendentals=2 * stations * window
        ),
        name="synthetics",
    )(
        in_hbm(rec_element.reshape(line)),
        in_hbm(rec_coords),
        blocks,
        starts,
        in_hbm(window_end.reshape(line)),
        in_hbm(point_traces),
    )

    partial, residual, other, factor = pl.pallas_call(
        misfit_kernel,
        out_shape=(
            pltpu.VMEM((slices, 1, LANES), f32),
            jax.ShapeDtypeStruct((COMPS, stations, window), f32),
            jax.ShapeDtypeStruct((TAPERS * COMPS * stations, LANES), f32),
            jax.ShapeDtypeStruct((stations, LANES), f32),
        ),
        in_specs=[far] + [whole()] * 5,
        out_specs=(whole(),) * 4,
        scratch_shapes=[
            pltpu.SMEM(line, i32),
            pltpu.VMEM((COMPS * stations * 2 * tiles, LANES), f32),
            pltpu.VMEM((TAPERS * COMPS * stations, LANES), f32),
            pltpu.SemaphoreType.DMA,
        ],
        compiler_params=params,
        cost_estimate=pl.CostEstimate(flops=1 << 24, bytes_accessed=3 << 20, transcendentals=0),
        name="misfit",
    )(blocks, columns, taken, synthetic, tapers, squares)
    partials = lax.all_to_all(partial, "cuts", split_axis=0, concat_axis=0, tiled=True)

    adjoint_points = pl.pallas_call(
        spread_kernel,
        out_shape=jax.ShapeDtypeStruct(point_traces.shape, point_traces.dtype),
        in_specs=[far] + [whole()] * 6,
        out_specs=far,
        scratch_shapes=[
            pltpu.SMEM(line, i32),
            pltpu.VMEM((tiles * step, LANES), f32),
            pltpu.VMEM(((samples // LANES + 1) * step, LANES), f32),
            pltpu.VMEM((COMPS, elements) + point_traces.shape[2:], bf16),
            pltpu.SemaphoreType.DMA((COMPS + 1,)),
        ],
        compiler_params=params,
        cost_estimate=pl.CostEstimate(
            flops=2 * 192 * 96 * 3 * samples, bytes_accessed=6 << 20, transcendentals=0
        ),
        name="spread_adjoint",
    )(starts, residual, tapers, squares, other, factor, spread_weights)

    total = jnp.sum(partials[:, 0, 0])
    total_misfit = jnp.reshape(total / (3.0 * window * stations * slices), (1,))
    return (adjoint_points, total_misfit)


def solution(mesh):
    return jax.shard_map(
        local,
        mesh=mesh,
        in_specs=(
            P(("event", "cuts"), None, None, None),
            P(("event", "cuts")),
            P(None, ("event", "cuts")),
            P(("event", "cuts"), None),
            P(("event", "cuts")),
            P(("event", "cuts")),
            P(("event", "cuts"), None, None),
        ),
        out_specs=(P(("event", "cuts"), None, None, None), P("event")),
        check_vma=False,
    )
```

```python
import functools
import math

import jax
import jax.numpy as jnp
from jax import lax
from jax.experimental import pallas as pl
from jax.experimental.pallas import tpu as pltpu
from jax.sharding import PartitionSpec as P

TAPERS = 5
NF = 512
COMPS = 3
LANES = 128
SUBLANES = 8
FACE = 25
FACE_PAD = 32
PIECE = 56
VMEM_LIMIT = 48 * 1024 * 1024
UNROLL = 8

gll_nodes = (-1.0, -0.6546536707079771, 0.0, 0.6546536707079771, 1.0)


def lagrange_values(coordinate):
    values = []
    for first_node in range(5):
        value = jnp.ones_like(coordinate)
        for other_node in range(5):
            if other_node != first_node:
                value = (
                    value
                    * (coordinate - gll_nodes[other_node])
                    / (gll_nodes[first_node] - gll_nodes[other_node])
                )
        values.append(value)
    return values


def choose(index, values):
    chosen = jnp.where(index == 0, values[0], 0.0)
    for at in range(1, len(values)):
        chosen = jnp.where(index == at, values[at], chosen)
    return chosen


def third_part(weights, part):
    high = weights.astype(jnp.bfloat16).astype(jnp.float32)
    middle = (weights - high).astype(jnp.bfloat16).astype(jnp.float32)
    low = weights - high - middle
    kept = jnp.where(part == 0, high, jnp.where(part == 1, middle, jnp.where(part == 2, low, 0.0)))
    return kept.astype(jnp.bfloat16)


def iota(shape, dim):
    return lax.broadcasted_iota(jnp.int32, shape, dim)


def pack_kernel(block_ref, obs_ref, out_ref, raw, names_vmem, rows, staged, tail, sems):
    pairs = out_ref.shape[0]
    tiles = obs_ref.shape[2] // LANES
    fetches = [pltpu.make_async_copy(obs_ref.at[comp], raw.at[comp], sems.at[comp]) for comp in range(COMPS)]
    fetches.append(pltpu.make_async_copy(block_ref, names_vmem, sems.at[COMPS]))
    for fetch in fetches:
        fetch.start()
    leave = [
        pltpu.make_async_copy(staged.at[comp], out_ref.at[:, 16 * comp : 16 * comp + 16, :], sems.at[COMPS + 1 + comp])
        for comp in range(COMPS)
    ]
    leave.append(pltpu.make_async_copy(tail, out_ref.at[:, 48:56, :], sems.at[2 * COMPS + 1]))
    for comp in range(COMPS):
        fetches[comp].wait()
        for tile in range(tiles):
            values = raw[comp, :, tile * LANES : (tile + 1) * LANES].astype(jnp.float32)
            rows[comp, pl.ds(tile, 2 * pairs, stride=tiles), :] = values
        for pair in range(pairs):
            staged[comp, pair] = rows[comp, 16 * pair : 16 * pair + 16, :].astype(jnp.bfloat16)
        leave[comp].start()
    fetches[COMPS].wait()
    column = as_column(names_vmem[...].astype(jnp.float32))
    hits = jnp.where(iota((pairs, LANES), 1).astype(jnp.float32) == column, 1.0, 0.0)
    histogram = jnp.sum(hits, axis=0, keepdims=True)
    last = jnp.where(iota((SUBLANES, LANES), 0) == 0, histogram, 0.0).astype(jnp.bfloat16)
    for pair in range(pairs):
        tail[pair] = last
    leave[COMPS].start()
    for copy in leave:
        copy.wait()


def as_column(row):
    square = (row.shape[1], row.shape[1])
    own = jnp.where(iota(square, 0) == iota(square, 1), jnp.broadcast_to(row, square), 0.0)
    return jnp.sum(own, axis=1, keepdims=True)


def as_row(column):
    tall = (column.shape[0], LANES)
    own = jnp.where(iota(tall, 0) == iota(tall, 1) % column.shape[0], jnp.broadcast_to(column, tall), 0.0)
    return jnp.sum(own, axis=0, keepdims=True)


def synth_kernel(
    element_ref, coords_ref, block_ref, start_ref, end_ref, traces_ref,
    syn_ref, taper_ref, square_ref, spread_ref, columns_ref, names_ref,
    element_vmem, coords_vmem, block_vmem, start_vmem, end_vmem, start_smem, traces, wide, moved, sems,
):
    elements = traces_ref.shape[0]
    stations = syn_ref.shape[1]
    window = syn_ref.shape[2]
    tiles = window // LANES
    all_tiles = traces_ref.shape[3] // LANES
    step = SUBLANES * stations
    pairs = [
        (element_ref, element_vmem), (coords_ref, coords_vmem), (block_ref, block_vmem),
        (start_ref, start_vmem), (end_ref, end_vmem), (start_ref, start_smem),
    ]
    small = [pltpu.make_async_copy(a, b, sems.at[at]) for at, (a, b) in enumerate(pairs)]
    large = [
        pltpu.make_async_copy(traces_ref.at[:, comp], traces.at[comp], sems.at[len(pairs) + comp])
        for comp in range(COMPS)
    ]
    for fetch in small + large:
        fetch.start()
    for fetch in small:
        fetch.wait()

    span_row = (end_vmem[...] - start_vmem[...]).astype(jnp.float32)
    name_row = block_vmem[...].astype(jnp.float32)
    xi = as_column(coords_vmem[0:1, :])
    eta = as_column(coords_vmem[1:2, :])
    element = as_column(element_vmem[...].astype(jnp.float32))
    span = as_column(span_row)
    name = as_column(name_row)
    square = (stations, stations)
    twin = (jnp.broadcast_to(name_row, square) == name) & (iota(square, 1) < iota(square, 0))
    rank = jnp.sum(jnp.where(twin, 1.0, 0.0), axis=1, keepdims=True)
    names_ref[...] = jnp.broadcast_to(name.astype(jnp.int32), names_ref.shape)
    columns_ref[...] = choose(iota((stations, LANES), 1), [span, name, rank])

    for tile in range(tiles):
        lanes = slice(tile * LANES, (tile + 1) * LANES)
        sample = iota((stations, LANES), 1).astype(jnp.float32) + float(tile * LANES)
        inside = sample < span
        angle = jnp.where(inside, math.pi * (sample + 1.0) / (span + 1.0), 0.0)
        first = math.sqrt(2.0) * jnp.sin(angle)
        twice = 2.0 * jnp.cos(angle)
        tapers = [jnp.where(inside, first, 0.0)]
        tapers.append(twice * tapers[0])
        for _ in range(2, TAPERS):
            tapers.append(twice * tapers[-1] - tapers[-2])
        squares = tapers[0] * tapers[0]
        taper_ref[0, :, lanes] = tapers[0]
        for order in range(1, TAPERS):
            taper_ref[order, :, lanes] = tapers[order]
            squares = squares + tapers[order] * tapers[order]
        square_ref[:, lanes] = float(NF) * squares

    height = elements * FACE_PAD
    face = iota((FACE_PAD, LANES), 0)
    along_xi = choose(face // 5, lagrange_values(as_row(xi)))
    along_eta = choose(face % 5, lagrange_values(as_row(eta)))
    weights = jnp.where(face < FACE, along_xi * along_eta, 0.0)
    thirds = third_part(weights, iota((FACE_PAD, LANES), 1) // stations).astype(jnp.float32)
    element_row = as_row(element)
    for at in range(elements):
        spread_ref[at * FACE_PAD : (at + 1) * FACE_PAD, :] = jnp.where(element_row == at, thirds, 0.0).astype(jnp.bfloat16)

    face = iota((stations, FACE_PAD), 1)
    along_xi = choose(face // 5, lagrange_values(xi))
    along_eta = choose(face % 5, lagrange_values(eta))
    weights = jnp.where(face < FACE, along_xi * along_eta, 0.0)
    by_station = [third_part(weights, part).astype(jnp.float32) for part in range(3)]
    by_station = jnp.concatenate(by_station, axis=0)
    elements_3 = jnp.concatenate([element, element, element], axis=0)
    here = [jnp.where(elements_3 == at, by_station, 0.0).astype(jnp.bfloat16)[:, :FACE] for at in range(elements)]

    for comp in range(COMPS):
        large[comp].wait()
        total = None
        for at in range(elements):
            term = jnp.dot(here[at], traces[comp, at], preferred_element_type=jnp.float32)
            total = term if total is None else total + term
        sampled = total[:stations] + total[stations : 2 * stations] + total[2 * stations : 3 * stations]
        for tile in range(all_tiles):
            wide[pl.ds(tile * step + comp, stations, stride=SUBLANES), :] = sampled[
                :, tile * LANES : (tile + 1) * LANES
            ]
    wide[all_tiles * step :, :] = jnp.zeros((step, LANES), jnp.float32)

    lane = iota((SUBLANES, LANES), 1)

    def cut(station, carry):
        start = start_smem[0, station]
        first = start // LANES
        shift = start % LANES
        back = (LANES - shift) % LANES
        keep = lane < LANES - shift
        turned = []
        for tile in range(tiles + 1):
            at = pl.multiple_of((first + tile) * step + station * SUBLANES, SUBLANES)
            turned.append(pltpu.roll(wide[pl.ds(at, SUBLANES), :], back, 1))
        for tile in range(tiles):
            at = pl.multiple_of(tile * step + station * SUBLANES, SUBLANES)
            moved[pl.ds(at, SUBLANES), :] = jnp.where(keep, turned[tile], turned[tile + 1])
        return carry

    lax.fori_loop(0, stations, cut, 0, unroll=UNROLL)

    for comp in range(COMPS):
        for tile in range(tiles):
            piece = moved[pl.ds(tile * step + comp, stations, stride=SUBLANES), :]
            syn_ref[comp, :, tile * LANES : (tile + 1) * LANES] = piece.astype(jnp.bfloat16).astype(jnp.float32)


def misfit_kernel(
    scale, block_ref, columns_ref, taken_ref, syn_ref, taper_ref, square_ref,
    partial_ref, residual_ref, other_ref, factor_ref, picked, sums,
):
    stations = columns_ref.shape[0]
    pairs = taken_ref.shape[0]
    window = syn_ref.shape[2]
    tiles = window // LANES
    columns = columns_ref[...]
    counts = taken_ref[0, 48:56, :].astype(jnp.float32)
    for pair in range(1, pairs):
        counts = counts + taken_ref[pair, 48:56, :].astype(jnp.float32)
    for station in range(stations):
        block = block_ref[station : station + 1, 0:1][0, 0]
        for comp in range(COMPS):
            at = (comp * stations + station) * 2 * tiles
            picked[at : at + 2 * tiles, :] = taken_ref[block, 16 * comp : 16 * comp + 16, :].astype(jnp.float32)
    name = columns[:, 1:2]
    lane_f = iota((stations, LANES), 1).astype(jnp.float32)
    count = jnp.sum(jnp.where(lane_f == name, counts[0:1, :], 0.0), axis=1, keepdims=True)

    lane = iota((SUBLANES, LANES), 1).astype(jnp.float32)
    energies, powers = [], []
    for group in range(stations // SUBLANES):
        rows = slice(group * SUBLANES, (group + 1) * SUBLANES)
        span = columns[rows, 0:1]
        second = columns[rows, 2:3] > 0.0
        energy = jnp.zeros((SUBLANES, LANES), jnp.float32)
        power = jnp.zeros((SUBLANES, LANES), jnp.float32)
        parts = [jnp.zeros((SUBLANES, LANES), jnp.float32) for _ in range(TAPERS * COMPS)]
        for tile in range(tiles):
            lanes = slice(tile * LANES, (tile + 1) * LANES)
            inside = lane + float(tile * LANES) < span
            observed, residual = [], []
            for comp in range(COMPS):
                at = (comp * stations + group * SUBLANES) * 2 * tiles + tile
                first_rank = picked[pl.ds(at, SUBLANES, stride=2 * tiles), :]
                second_rank = picked[pl.ds(at + tiles, SUBLANES, stride=2 * tiles), :]
                observed.append(jnp.where(second, second_rank, first_rank))
                residual.append(syn_ref[comp, rows, lanes] - observed[comp])
                residual_ref[comp, rows, lanes] = residual[comp]
            squares = observed[0] * observed[0] + observed[1] * observed[1] + observed[2] * observed[2]
            energy = energy + jnp.where(inside, squares, 0.0)
            squares = residual[0] * residual[0] + residual[1] * residual[1] + residual[2] * residual[2]
            power = power + square_ref[rows, lanes] * squares
            for order in range(TAPERS):
                taper = taper_ref[order, rows, lanes]
                for comp in range(COMPS):
                    at = order * COMPS + comp
                    parts[at] = parts[at] + taper * residual[comp]
        for at in range(TAPERS * COMPS):
            start = at * stations + group * SUBLANES
            sums[start : start + SUBLANES, :] = parts[at]
        energies.append(energy)
        powers.append(power)

    odd = (iota((LANES, LANES), 0) + iota((LANES, LANES), 1)) % 2
    odd = odd.astype(jnp.float32).astype(jnp.bfloat16)
    whole = sums[...]
    high = whole.astype(jnp.bfloat16)
    low = (whole - high.astype(jnp.float32)).astype(jnp.bfloat16)
    other = jnp.dot(high, odd, preferred_element_type=jnp.float32) + jnp.dot(
        low, odd, preferred_element_type=jnp.float32
    )
    other_ref[...] = other
    product = whole * other
    power = jnp.concatenate(powers, axis=0)
    for at in range(TAPERS * COMPS):
        power = power + product[at * stations : (at + 1) * stations]
    energy = jnp.sum(jnp.concatenate(energies, axis=0), axis=1, keepdims=True)
    power = jnp.sum(power, axis=1, keepdims=True)
    energy = energy / (3.0 * columns[:, 0:1]) + 1e-05
    weight = float(stations) / count
    factor = weight / (float(TAPERS * NF) * energy)
    factor_ref[...] = jnp.broadcast_to(factor, factor_ref.shape)
    partial = jnp.sum(scale * (factor * power), axis=0, keepdims=True)
    partial_ref[...] = jnp.broadcast_to(partial[:, :, None], partial_ref.shape)


def spread_kernel(
    start_ref, residual_ref, taper_ref, square_ref, other_ref, factor_ref, spread_ref,
    out_ref, start_smem, source, placed, staged, sems,
):
    fetch = pltpu.make_async_copy(start_ref, start_smem, sems.at[COMPS])
    fetch.start()
    elements = out_ref.shape[0]
    stations = factor_ref.shape[0]
    tiles = residual_ref.shape[2] // LANES
    all_tiles = out_ref.shape[3] // LANES
    step = SUBLANES * stations
    for comp in range(COMPS):
        for group in range(stations // SUBLANES):
            rows = slice(group * SUBLANES, (group + 1) * SUBLANES)
            factor = factor_ref[rows, :]
            for tile in range(tiles):
                lanes = slice(tile * LANES, (tile + 1) * LANES)
                value = square_ref[rows, lanes] * residual_ref[comp, rows, lanes]
                for order in range(TAPERS):
                    at = (order * COMPS + comp) * stations + group * SUBLANES
                    value = value + taper_ref[order, rows, lanes] * other_ref[at : at + SUBLANES, :]
                value = (factor * value).astype(jnp.bfloat16).astype(jnp.float32)
                at = tile * step + group * SUBLANES * SUBLANES + comp
                source[pl.ds(at, SUBLANES, stride=SUBLANES), :] = value

    placed[...] = jnp.zeros(placed.shape, jnp.float32)
    lane = iota((SUBLANES, LANES), 1)

    fetch.wait()

    def put(station, carry):
        start = start_smem[0, station]
        first = start // LANES
        shift = start % LANES
        keep = lane >= shift
        turned = [jnp.zeros((SUBLANES, LANES), jnp.float32)]
        for tile in range(tiles):
            at = pl.multiple_of(tile * step + station * SUBLANES, SUBLANES)
            turned.append(pltpu.roll(source[pl.ds(at, SUBLANES), :], shift, 1))
        turned.append(turned[0])
        for tile in range(tiles + 1):
            at = pl.multiple_of((first + tile) * step + station * SUBLANES, SUBLANES)
            placed[pl.ds(at, SUBLANES), :] = jnp.where(keep, turned[tile + 1], turned[tile])
        return carry

    lax.fori_loop(0, stations, put, 0, unroll=UNROLL)

    weights = spread_ref[:, : 3 * stations]
    for comp in range(COMPS):
        pieces = []
        for tile in range(all_tiles):
            piece = placed[pl.ds(tile * step + comp, stations, stride=SUBLANES), :]
            pieces.append(piece.astype(jnp.bfloat16))
        values = jnp.concatenate(pieces, axis=1)
        values = jnp.concatenate([values, values, values], axis=0)
        result = jnp.dot(weights, values, preferred_element_type=jnp.float32)
        for at in range(elements):
            rows = slice(at * FACE_PAD, at * FACE_PAD + FACE)
            staged[comp, at, :, :] = result[rows].astype(staged.dtype)
        pltpu.make_async_copy(staged.at[comp], out_ref.at[:, comp], sems.at[comp]).start()
    for comp in range(COMPS):
        pltpu.make_async_copy(staged.at[comp], out_ref.at[:, comp], sems.at[comp]).wait()


def whole(space=pltpu.VMEM):
    return pl.BlockSpec(memory_space=space)


def in_hbm(array):
    return pltpu.with_memory_space_constraint(array, pltpu.HBM)


def local(point_traces, rec_element, rec_coords, slot_block, window_start, window_end, obs_windows):
    slices = lax.axis_size("cuts")
    stations = rec_element.shape[0]
    window = obs_windows.shape[2]
    tiles = window // LANES
    samples = point_traces.shape[3]
    elements = point_traces.shape[0]
    line = (1, stations)
    blocks = in_hbm(slot_block.reshape(line))
    starts = in_hbm(window_start.reshape(line))
    params = pltpu.CompilerParams(vmem_limit_bytes=VMEM_LIMIT)
    f32, i32, bf16 = jnp.float32, jnp.int32, jnp.bfloat16
    far = whole(pltpu.HBM)

    packed = pl.pallas_call(
        pack_kernel,
        out_shape=jax.ShapeDtypeStruct((slices, PIECE, LANES), bf16),
        in_specs=[far, far],
        out_specs=far,
        scratch_shapes=[
            pltpu.VMEM((COMPS, obs_windows.shape[0], window), bf16),
            pltpu.VMEM(line, i32),
            pltpu.VMEM((COMPS, obs_windows.shape[0] * tiles, LANES), f32),
            pltpu.VMEM((COMPS, slices, 16, LANES), bf16),
            pltpu.VMEM((slices, SUBLANES, LANES), bf16),
            pltpu.SemaphoreType.DMA((2 * (COMPS + 1),)),
        ],
        compiler_params=params,
        cost_estimate=pl.CostEstimate(flops=0, bytes_accessed=1 << 20, transcendentals=0),
        name="pack_observed",
    )(blocks, in_hbm(jnp.transpose(obs_windows, (1, 0, 2))))
    taken = lax.all_to_all(packed, "cuts", split_axis=0, concat_axis=0, tiled=True)

    step = SUBLANES * stations
    synthetic, tapers, squares, spread_weights, columns, names = pl.pallas_call(
        synth_kernel,
        out_shape=(
            jax.ShapeDtypeStruct((COMPS, stations, window), f32),
            jax.ShapeDtypeStruct((TAPERS, stations, window), f32),
            jax.ShapeDtypeStruct((stations, window), f32),
            jax.ShapeDtypeStruct((elements * FACE_PAD, LANES), bf16),
            jax.ShapeDtypeStruct((stations, LANES), f32),
            jax.ShapeDtypeStruct((stations, LANES), i32),
        ),
        in_specs=[far] * 6,
        out_specs=(whole(),) * 6,
        scratch_shapes=[
            pltpu.VMEM(line, i32),
            pltpu.VMEM((2, stations), f32),
            pltpu.VMEM(line, i32),
            pltpu.VMEM(line, i32),
            pltpu.VMEM(line, i32),
            pltpu.SMEM(line, i32),
            pltpu.VMEM((COMPS, elements) + point_traces.shape[2:], bf16),
            pltpu.VMEM(((samples // LANES + 1) * step, LANES), f32),
            pltpu.VMEM((tiles * step, LANES), f32),
            pltpu.SemaphoreType.DMA((6 + COMPS,)),
        ],
        compiler_params=params,
        cost_estimate=pl.CostEstimate(
            flops=2 * 96 * 32 * 18 * samples, bytes_accessed=4 << 20, transcendentals=2 * stations * window
        ),
        name="synthetics",
    )(
        in_hbm(rec_element.reshape(line)),
        in_hbm(rec_coords),
        blocks,
        starts,
        in_hbm(window_end.reshape(line)),
        in_hbm(point_traces),
    )

    partial, residual, other, factor = pl.pallas_call(
        functools.partial(misfit_kernel, 0.5 / (3.0 * window * stations * slices)),
        out_shape=(
            pltpu.VMEM((slices, 1, LANES), f32),
            jax.ShapeDtypeStruct((COMPS, stations, window), f32),
            jax.ShapeDtypeStruct((TAPERS * COMPS * stations, LANES), f32),
            jax.ShapeDtypeStruct((stations, LANES), f32),
        ),
        in_specs=[whole()] * 6,
        out_specs=(whole(),) * 4,
        scratch_shapes=[
            pltpu.VMEM((COMPS * stations * 2 * tiles, LANES), f32),
            pltpu.VMEM((TAPERS * COMPS * stations, LANES), f32),
        ],
        compiler_params=params,
        cost_estimate=pl.CostEstimate(flops=1 << 24, bytes_accessed=3 << 20, transcendentals=0),
        name="misfit",
    )(names, columns, taken, synthetic, tapers, squares)
    partials = lax.all_to_all(partial, "cuts", split_axis=0, concat_axis=0, tiled=True)

    adjoint_points = pl.pallas_call(
        spread_kernel,
        out_shape=jax.ShapeDtypeStruct(point_traces.shape, point_traces.dtype),
        in_specs=[far] + [whole()] * 6,
        out_specs=far,
        scratch_shapes=[
            pltpu.SMEM(line, i32),
            pltpu.VMEM((tiles * step, LANES), f32),
            pltpu.VMEM(((samples // LANES + 1) * step, LANES), f32),
            pltpu.VMEM((COMPS, elements) + point_traces.shape[2:], bf16),
            pltpu.SemaphoreType.DMA((COMPS + 1,)),
        ],
        compiler_params=params,
        cost_estimate=pl.CostEstimate(
            flops=2 * 192 * 96 * 3 * samples, bytes_accessed=6 << 20, transcendentals=0
        ),
        name="spread_adjoint",
    )(starts, residual, tapers, squares, other, factor, spread_weights)

    total_misfit = jnp.sum(partials[:, 0, :1], axis=0)
    return (adjoint_points, total_misfit)


def solution(mesh):
    return jax.shard_map(
        local,
        mesh=mesh,
        in_specs=(
            P(("event", "cuts"), None, None, None),
            P(("event", "cuts")),
            P(None, ("event", "cuts")),
            P(("event", "cuts"), None),
            P(("event", "cuts")),
            P(("event", "cuts")),
            P(("event", "cuts"), None, None),
        ),
        out_specs=(P(("event", "cuts"), None, None, None), P("event")),
        check_vma=False,
    )
```

```python
import functools
import math

import jax
import jax.numpy as jnp
from jax import lax
from jax.experimental import pallas as pl
from jax.experimental.pallas import tpu as pltpu
from jax.sharding import PartitionSpec as P

TAPERS = 5
NF = 512
COMPS = 3
LANES = 128
SUBLANES = 8
FACE = 25
FACE_PAD = 32
PIECE = 50
VMEM_LIMIT = 48 * 1024 * 1024
UNROLL = 8

gll_nodes = (-1.0, -0.6546536707079771, 0.0, 0.6546536707079771, 1.0)


def lagrange_values(coordinate):
    values = []
    for first_node in range(5):
        value = jnp.ones_like(coordinate)
        for other_node in range(5):
            if other_node != first_node:
                value = (
                    value
                    * (coordinate - gll_nodes[other_node])
                    / (gll_nodes[first_node] - gll_nodes[other_node])
                )
        values.append(value)
    return values


def choose(index, values):
    chosen = jnp.where(index == 0, values[0], 0.0)
    for at in range(1, len(values)):
        chosen = jnp.where(index == at, values[at], chosen)
    return chosen


def third_part(weights, part):
    high = weights.astype(jnp.bfloat16).astype(jnp.float32)
    middle = (weights - high).astype(jnp.bfloat16).astype(jnp.float32)
    low = weights - high - middle
    kept = jnp.where(part == 0, high, jnp.where(part == 1, middle, jnp.where(part == 2, low, 0.0)))
    return kept.astype(jnp.bfloat16)


def iota(shape, dim):
    return lax.broadcasted_iota(jnp.int32, shape, dim)


def pack_kernel(block_ref, obs_ref, out_ref, raw, names_vmem, flat, rows, staged, sems):
    pairs = obs_ref.shape[1] // 2
    tiles = obs_ref.shape[2] // LANES
    fetches = [pltpu.make_async_copy(obs_ref.at[comp], raw.at[comp], sems.at[comp]) for comp in range(COMPS)]
    fetches.append(pltpu.make_async_copy(block_ref, names_vmem, sems.at[COMPS]))
    for fetch in fetches:
        fetch.start()
    half = rows.shape[0] // 2
    leave = [
        pltpu.make_async_copy(
            staged.at[half * part : half * (part + 1)],
            out_ref.at[half * part : half * (part + 1)],
            sems.at[COMPS + 1 + part],
        )
        for part in range(2)
    ]
    for comp in range(COMPS):
        fetches[comp].wait()
        for tile in range(tiles):
            at = (comp * tiles + tile) * 2 * pairs
            flat[at : at + 2 * pairs, :] = raw[comp, :, tile * LANES : (tile + 1) * LANES].astype(jnp.float32)
            for rank in range(2):
                values = flat[pl.ds(at + rank, pairs, stride=2), :]
                rows[pl.ds((comp * 2 + rank) * tiles + tile, pairs, stride=PIECE), :] = values
    fetches[COMPS].wait()
    column = as_column(names_vmem[...].astype(jnp.float32))
    hits = jnp.where(iota((pairs, LANES), 1).astype(jnp.float32) == column, 1.0, 0.0)
    histogram = jnp.sum(hits, axis=0, keepdims=True)
    rows[pl.ds(PIECE - 2, pairs, stride=PIECE), :] = jnp.broadcast_to(histogram, (pairs, LANES))
    rows[pl.ds(PIECE - 1, pairs, stride=PIECE), :] = jnp.zeros((pairs, LANES), jnp.float32)
    for part in range(2):
        own = slice(half * part, half * (part + 1))
        staged[own, :] = rows[own, :].astype(jnp.bfloat16)
        leave[part].start()
    for copy in leave:
        copy.wait()


def as_column(row):
    square = (row.shape[1], row.shape[1])
    own = jnp.where(iota(square, 0) == iota(square, 1), jnp.broadcast_to(row, square), 0.0)
    return jnp.sum(own, axis=1, keepdims=True)


def as_row(column):
    tall = (column.shape[0], LANES)
    own = jnp.where(iota(tall, 0) == iota(tall, 1) % column.shape[0], jnp.broadcast_to(column, tall), 0.0)
    return jnp.sum(own, axis=0, keepdims=True)


def synth_kernel(
    element_ref, coords_ref, block_ref, start_ref, end_ref, traces_ref,
    syn_ref, taper_ref, square_ref, spread_ref, columns_ref, places_ref,
    element_vmem, coords_vmem, block_vmem, start_vmem, end_vmem, start_smem, traces, wide, moved, sems,
):
    elements = traces_ref.shape[0]
    stations = syn_ref.shape[1]
    window = syn_ref.shape[2]
    tiles = window // LANES
    all_tiles = traces_ref.shape[3] // LANES
    step = SUBLANES * stations
    pairs = [
        (element_ref, element_vmem), (coords_ref, coords_vmem), (block_ref, block_vmem),
        (start_ref, start_vmem), (end_ref, end_vmem), (start_ref, start_smem),
    ]
    small = [pltpu.make_async_copy(a, b, sems.at[at]) for at, (a, b) in enumerate(pairs)]
    large = [
        pltpu.make_async_copy(traces_ref.at[:, comp], traces.at[comp], sems.at[len(pairs) + comp])
        for comp in range(COMPS)
    ]
    for fetch in small + large:
        fetch.start()
    for fetch in small:
        fetch.wait()

    span_row = (end_vmem[...] - start_vmem[...]).astype(jnp.float32)
    name_row = block_vmem[...].astype(jnp.float32)
    xi = as_column(coords_vmem[0:1, :])
    eta = as_column(coords_vmem[1:2, :])
    element = as_column(element_vmem[...].astype(jnp.float32))
    span = as_column(span_row)
    name = as_column(name_row)
    square = (stations, stations)
    twin = (jnp.broadcast_to(name_row, square) == name) & (iota(square, 1) < iota(square, 0))
    rank = jnp.sum(jnp.where(twin, 1.0, 0.0), axis=1, keepdims=True)
    first_row = (float(PIECE) * name + float(tiles) * rank).astype(jnp.int32)
    places_ref[...] = jnp.broadcast_to(first_row, places_ref.shape)
    columns_ref[...] = choose(iota((stations, LANES), 1), [span, name])

    for tile in range(tiles):
        lanes = slice(tile * LANES, (tile + 1) * LANES)
        sample = iota((stations, LANES), 1).astype(jnp.float32) + float(tile * LANES)
        inside = sample < span
        angle = jnp.where(inside, math.pi * (sample + 1.0) / (span + 1.0), 0.0)
        first = math.sqrt(2.0) * jnp.sin(angle)
        twice = 2.0 * jnp.cos(angle)
        tapers = [jnp.where(inside, first, 0.0)]
        tapers.append(twice * tapers[0])
        for _ in range(2, TAPERS):
            tapers.append(twice * tapers[-1] - tapers[-2])
        squares = tapers[0] * tapers[0]
        taper_ref[0, :, lanes] = tapers[0]
        for order in range(1, TAPERS):
            taper_ref[order, :, lanes] = tapers[order]
            squares = squares + tapers[order] * tapers[order]
        square_ref[:, lanes] = float(NF) * squares

    height = elements * FACE_PAD
    face = iota((FACE_PAD, LANES), 0)
    along_xi = choose(face // 5, lagrange_values(as_row(xi)))
    along_eta = choose(face % 5, lagrange_values(as_row(eta)))
    weights = jnp.where(face < FACE, along_xi * along_eta, 0.0)
    thirds = third_part(weights, iota((FACE_PAD, LANES), 1) // stations).astype(jnp.float32)
    element_row = as_row(element)
    for at in range(elements):
        spread_ref[at * FACE_PAD : (at + 1) * FACE_PAD, :] = jnp.where(element_row == at, thirds, 0.0).astype(jnp.bfloat16)

    face = iota((stations, FACE_PAD), 1)
    along_xi = choose(face // 5, lagrange_values(xi))
    along_eta = choose(face % 5, lagrange_values(eta))
    weights = jnp.where(face < FACE, along_xi * along_eta, 0.0)
    by_station = [third_part(weights, part).astype(jnp.float32) for part in range(3)]
    by_station = jnp.concatenate(by_station, axis=0)
    elements_3 = jnp.concatenate([element, element, element], axis=0)
    here = [jnp.where(elements_3 == at, by_station, 0.0).astype(jnp.bfloat16)[:, :FACE] for at in range(elements)]

    for comp in range(COMPS):
        large[comp].wait()
        total = None
        for at in range(elements):
            term = jnp.dot(here[at], traces[comp, at], preferred_element_type=jnp.float32)
            total = term if total is None else total + term
        sampled = total[:stations] + total[stations : 2 * stations] + total[2 * stations : 3 * stations]
        for tile in range(all_tiles):
            wide[pl.ds(tile * step + comp, stations, stride=SUBLANES), :] = sampled[
                :, tile * LANES : (tile + 1) * LANES
            ]
    wide[all_tiles * step :, :] = jnp.zeros((step, LANES), jnp.float32)

    lane = iota((SUBLANES, LANES), 1)

    def cut(station, carry):
        start = start_smem[0, station]
        first = start // LANES
        shift = start % LANES
        back = (LANES - shift) % LANES
        keep = lane < LANES - shift
        turned = []
        for tile in range(tiles + 1):
            at = pl.multiple_of((first + tile) * step + station * SUBLANES, SUBLANES)
            turned.append(pltpu.roll(wide[pl.ds(at, SUBLANES), :], back, 1))
        for tile in range(tiles):
            at = pl.multiple_of(tile * step + station * SUBLANES, SUBLANES)
            moved[pl.ds(at, SUBLANES), :] = jnp.where(keep, turned[tile], turned[tile + 1])
        return carry

    lax.fori_loop(0, stations, cut, 0, unroll=UNROLL)

    for comp in range(COMPS):
        for tile in range(tiles):
            piece = moved[pl.ds(tile * step + comp, stations, stride=SUBLANES), :]
            syn_ref[comp, :, tile * LANES : (tile + 1) * LANES] = piece.astype(jnp.bfloat16).astype(jnp.float32)


def misfit_kernel(
    scale, place_ref, columns_ref, taken_ref, syn_ref, taper_ref, square_ref,
    partial_ref, residual_ref, other_ref, factor_ref, rows, picked, sums,
):
    stations = columns_ref.shape[0]
    pairs = taken_ref.shape[0] // PIECE
    window = syn_ref.shape[2]
    tiles = window // LANES
    columns = columns_ref[...]
    rows[...] = taken_ref[...].astype(jnp.float32)
    for station in range(stations):
        place = place_ref[station : station + 1, 0:1][0, 0]
        for comp in range(COMPS):
            at = (comp * stations + station) * tiles
            picked[at : at + tiles, :] = rows[pl.ds(place + 2 * tiles * comp, tiles), :]
    counts = jnp.sum(rows[pl.ds(PIECE - 2, pairs, stride=PIECE), :], axis=0, keepdims=True)
    name = columns[:, 1:2]
    lane_f = iota((stations, LANES), 1).astype(jnp.float32)
    count = jnp.sum(jnp.where(lane_f == name, counts, 0.0), axis=1, keepdims=True)

    lane = iota((SUBLANES, LANES), 1).astype(jnp.float32)
    energies, powers = [], []
    for group in range(stations // SUBLANES):
        own = slice(group * SUBLANES, (group + 1) * SUBLANES)
        span = columns[own, 0:1]
        energy = jnp.zeros((SUBLANES, LANES), jnp.float32)
        power = jnp.zeros((SUBLANES, LANES), jnp.float32)
        parts = [jnp.zeros((SUBLANES, LANES), jnp.float32) for _ in range(TAPERS * COMPS)]
        for tile in range(tiles):
            lanes = slice(tile * LANES, (tile + 1) * LANES)
            inside = lane + float(tile * LANES) < span
            observed, residual = [], []
            for comp in range(COMPS):
                at = (comp * stations + group * SUBLANES) * tiles + tile
                observed.append(picked[pl.ds(at, SUBLANES, stride=tiles), :])
                residual.append(syn_ref[comp, own, lanes] - observed[comp])
                residual_ref[comp, own, lanes] = residual[comp]
            squares = observed[0] * observed[0] + observed[1] * observed[1] + observed[2] * observed[2]
            energy = energy + jnp.where(inside, squares, 0.0)
            squares = residual[0] * residual[0] + residual[1] * residual[1] + residual[2] * residual[2]
            power = power + square_ref[own, lanes] * squares
            for order in range(TAPERS):
                taper = taper_ref[order, own, lanes]
                for comp in range(COMPS):
                    at = order * COMPS + comp
                    parts[at] = parts[at] + taper * residual[comp]
        for at in range(TAPERS * COMPS):
            start = at * stations + group * SUBLANES
            sums[start : start + SUBLANES, :] = parts[at]
        energies.append(energy)
        powers.append(power)

    odd = (iota((LANES, LANES), 0) + iota((LANES, LANES), 1)) % 2
    odd = odd.astype(jnp.float32).astype(jnp.bfloat16)
    whole = sums[...]
    high = whole.astype(jnp.bfloat16)
    low = (whole - high.astype(jnp.float32)).astype(jnp.bfloat16)
    other = jnp.dot(high, odd, preferred_element_type=jnp.float32) + jnp.dot(
        low, odd, preferred_element_type=jnp.float32
    )
    other_ref[...] = other
    product = whole * other
    power = jnp.concatenate(powers, axis=0)
    for at in range(TAPERS * COMPS):
        power = power + product[at * stations : (at + 1) * stations]
    energy = jnp.sum(jnp.concatenate(energies, axis=0), axis=1, keepdims=True)
    power = jnp.sum(power, axis=1, keepdims=True)
    energy = energy / (3.0 * columns[:, 0:1]) + 1e-05
    weight = float(stations) / count
    factor = weight / (float(TAPERS * NF) * energy)
    factor_ref[...] = jnp.broadcast_to(factor, factor_ref.shape)
    partial = jnp.sum(scale * (factor * power), axis=0, keepdims=True)
    partial_ref[...] = jnp.broadcast_to(partial[:, :, None], partial_ref.shape)


def spread_kernel(
    start_ref, residual_ref, taper_ref, square_ref, other_ref, factor_ref, spread_ref,
    out_ref, start_smem, source, placed, staged, sems,
):
    fetch = pltpu.make_async_copy(start_ref, start_smem, sems.at[COMPS])
    fetch.start()
    elements = out_ref.shape[0]
    stations = factor_ref.shape[0]
    tiles = residual_ref.shape[2] // LANES
    all_tiles = out_ref.shape[3] // LANES
    step = SUBLANES * stations
    for comp in range(COMPS):
        for group in range(stations // SUBLANES):
            rows = slice(group * SUBLANES, (group + 1) * SUBLANES)
            factor = factor_ref[rows, :]
            for tile in range(tiles):
                lanes = slice(tile * LANES, (tile + 1) * LANES)
                value = square_ref[rows, lanes] * residual_ref[comp, rows, lanes]
                for order in range(TAPERS):
                    at = (order * COMPS + comp) * stations + group * SUBLANES
                    value = value + taper_ref[order, rows, lanes] * other_ref[at : at + SUBLANES, :]
                value = (factor * value).astype(jnp.bfloat16).astype(jnp.float32)
                at = tile * step + group * SUBLANES * SUBLANES + comp
                source[pl.ds(at, SUBLANES, stride=SUBLANES), :] = value

    placed[...] = jnp.zeros(placed.shape, jnp.float32)
    lane = iota((SUBLANES, LANES), 1)

    fetch.wait()

    def put(station, carry):
        start = start_smem[0, station]
        first = start // LANES
        shift = start % LANES
        keep = lane >= shift
        turned = [jnp.zeros((SUBLANES, LANES), jnp.float32)]
        for tile in range(tiles):
            at = pl.multiple_of(tile * step + station * SUBLANES, SUBLANES)
            turned.append(pltpu.roll(source[pl.ds(at, SUBLANES), :], shift, 1))
        turned.append(turned[0])
        for tile in range(tiles + 1):
            at = pl.multiple_of((first + tile) * step + station * SUBLANES, SUBLANES)
            placed[pl.ds(at, SUBLANES), :] = jnp.where(keep, turned[tile + 1], turned[tile])
        return carry

    lax.fori_loop(0, stations, put, 0, unroll=UNROLL)

    weights = spread_ref[:, : 3 * stations]
    for comp in range(COMPS):
        pieces = []
        for tile in range(all_tiles):
            piece = placed[pl.ds(tile * step + comp, stations, stride=SUBLANES), :]
            pieces.append(piece.astype(jnp.bfloat16))
        values = jnp.concatenate(pieces, axis=1)
        values = jnp.concatenate([values, values, values], axis=0)
        result = jnp.dot(weights, values, preferred_element_type=jnp.float32)
        for at in range(elements):
            rows = slice(at * FACE_PAD, at * FACE_PAD + FACE)
            staged[comp, at, :, :] = result[rows].astype(staged.dtype)
        pltpu.make_async_copy(staged.at[comp], out_ref.at[:, comp], sems.at[comp]).start()
    for comp in range(COMPS):
        pltpu.make_async_copy(staged.at[comp], out_ref.at[:, comp], sems.at[comp]).wait()


def whole(space=pltpu.VMEM):
    return pl.BlockSpec(memory_space=space)


def in_hbm(array):
    return pltpu.with_memory_space_constraint(array, pltpu.HBM)


def local(point_traces, rec_element, rec_coords, slot_block, window_start, window_end, obs_windows):
    slices = lax.axis_size("cuts")
    stations = rec_element.shape[0]
    window = obs_windows.shape[2]
    tiles = window // LANES
    samples = point_traces.shape[3]
    elements = point_traces.shape[0]
    line = (1, stations)
    blocks = in_hbm(slot_block.reshape(line))
    starts = in_hbm(window_start.reshape(line))
    params = pltpu.CompilerParams(vmem_limit_bytes=VMEM_LIMIT)
    f32, i32, bf16 = jnp.float32, jnp.int32, jnp.bfloat16
    far = whole(pltpu.HBM)

    packed = pl.pallas_call(
        pack_kernel,
        out_shape=jax.ShapeDtypeStruct((slices * PIECE, LANES), bf16),
        in_specs=[far, far],
        out_specs=far,
        scratch_shapes=[
            pltpu.VMEM((COMPS, obs_windows.shape[0], window), bf16),
            pltpu.VMEM(line, i32),
            pltpu.VMEM((COMPS * tiles * obs_windows.shape[0], LANES), f32),
            pltpu.VMEM((slices * PIECE, LANES), f32),
            pltpu.VMEM((slices * PIECE, LANES), bf16),
            pltpu.SemaphoreType.DMA((COMPS + 3,)),
        ],
        compiler_params=params,
        cost_estimate=pl.CostEstimate(flops=0, bytes_accessed=1 << 20, transcendentals=0),
        name="pack_observed",
    )(blocks, in_hbm(jnp.transpose(obs_windows, (1, 0, 2))))
    packed = packed.reshape(slices, PIECE // 2, 2, LANES)
    taken = lax.all_to_all(packed, "cuts", split_axis=0, concat_axis=0, tiled=True)
    taken = taken.reshape(slices * PIECE, LANES)

    step = SUBLANES * stations
    synthetic, tapers, squares, spread_weights, columns, places = pl.pallas_call(
        synth_kernel,
        out_shape=(
            jax.ShapeDtypeStruct((COMPS, stations, window), f32),
            jax.ShapeDtypeStruct((TAPERS, stations, window), f32),
            jax.ShapeDtypeStruct((stations, window), f32),
            jax.ShapeDtypeStruct((elements * FACE_PAD, LANES), bf16),
            jax.ShapeDtypeStruct((stations, LANES), f32),
            jax.ShapeDtypeStruct((stations, LANES), i32),
        ),
        in_specs=[far] * 6,
        out_specs=(whole(),) * 6,
        scratch_shapes=[
            pltpu.VMEM(line, i32),
            pltpu.VMEM((2, stations), f32),
            pltpu.VMEM(line, i32),
            pltpu.VMEM(line, i32),
            pltpu.VMEM(line, i32),
            pltpu.SMEM(line, i32),
            pltpu.VMEM((COMPS, elements) + point_traces.shape[2:], bf16),
            pltpu.VMEM(((samples // LANES + 1) * step, LANES), f32),
            pltpu.VMEM((tiles * step, LANES), f32),
            pltpu.SemaphoreType.DMA((6 + COMPS,)),
        ],
        compiler_params=params,
        cost_estimate=pl.CostEstimate(
            flops=2 * 96 * 32 * 18 * samples, bytes_accessed=4 << 20, transcendentals=2 * stations * window
        ),
        name="synthetics",
    )(
        in_hbm(rec_element.reshape(line)),
        in_hbm(rec_coords),
        blocks,
        starts,
        in_hbm(window_end.reshape(line)),
        in_hbm(point_traces),
    )

    partial, residual, other, factor = pl.pallas_call(
        functools.partial(misfit_kernel, 0.5 / (3.0 * window * stations * slices)),
        out_shape=(
            pltpu.VMEM((slices, 1, LANES), f32),
            jax.ShapeDtypeStruct((COMPS, stations, window), f32),
            jax.ShapeDtypeStruct((TAPERS * COMPS * stations, LANES), f32),
            jax.ShapeDtypeStruct((stations, LANES), f32),
        ),
        in_specs=[whole()] * 6,
        out_specs=(whole(),) * 4,
        scratch_shapes=[
            pltpu.VMEM((slices * PIECE, LANES), f32),
            pltpu.VMEM((COMPS * stations * tiles, LANES), f32),
            pltpu.VMEM((TAPERS * COMPS * stations, LANES), f32),
        ],
        compiler_params=params,
        cost_estimate=pl.CostEstimate(flops=1 << 24, bytes_accessed=3 << 20, transcendentals=0),
        name="misfit",
    )(places, columns, taken, synthetic, tapers, squares)
    partials = lax.all_to_all(partial, "cuts", split_axis=0, concat_axis=0, tiled=True)

    adjoint_points = pl.pallas_call(
        spread_kernel,
        out_shape=jax.ShapeDtypeStruct(point_traces.shape, point_traces.dtype),
        in_specs=[far] + [whole()] * 6,
        out_specs=far,
        scratch_shapes=[
            pltpu.SMEM(line, i32),
            pltpu.VMEM((tiles * step, LANES), f32),
            pltpu.VMEM(((samples // LANES + 1) * step, LANES), f32),
            pltpu.VMEM((COMPS, elements) + point_traces.shape[2:], bf16),
            pltpu.SemaphoreType.DMA((COMPS + 1,)),
        ],
        compiler_params=params,
        cost_estimate=pl.CostEstimate(
            flops=2 * 192 * 96 * 3 * samples, bytes_accessed=6 << 20, transcendentals=0
        ),
        name="spread_adjoint",
    )(starts, residual, tapers, squares, other, factor, spread_weights)

    total_misfit = jnp.sum(partials[:, 0, :1], axis=0)
    return (adjoint_points, total_misfit)


def solution(mesh):
    return jax.shard_map(
        local,
        mesh=mesh,
        in_specs=(
            P(("event", "cuts"), None, None, None),
            P(("event", "cuts")),
            P(None, ("event", "cuts")),
            P(("event", "cuts"), None),
            P(("event", "cuts")),
            P(("event", "cuts")),
            P(("event", "cuts"), None, None),
        ),
        out_specs=(P(("event", "cuts"), None, None, None), P("event")),
        check_vma=False,
    )
```

```python
import functools
import math

import jax
import jax.numpy as jnp
from jax import lax
from jax.experimental import pallas as pl
from jax.experimental.pallas import tpu as pltpu
from jax.sharding import PartitionSpec as P

TAPERS = 5
NF = 512
COMPS = 3
LANES = 128
SUBLANES = 8
FACE = 25
FACE_PAD = 32
PIECE = 50
LAST = 64
VMEM_LIMIT = 48 * 1024 * 1024
UNROLL = 8

gll_nodes = (-1.0, -0.6546536707079771, 0.0, 0.6546536707079771, 1.0)


def lagrange_values(coordinate):
    values = []
    for first_node in range(5):
        value = jnp.ones_like(coordinate)
        for other_node in range(5):
            if other_node != first_node:
                value = (
                    value
                    * (coordinate - gll_nodes[other_node])
                    / (gll_nodes[first_node] - gll_nodes[other_node])
                )
        values.append(value)
    return values


def choose(index, values):
    chosen = jnp.where(index == 0, values[0], 0.0)
    for at in range(1, len(values)):
        chosen = jnp.where(index == at, values[at], chosen)
    return chosen


def third_part(weights, part):
    high = weights.astype(jnp.bfloat16).astype(jnp.float32)
    middle = (weights - high).astype(jnp.bfloat16).astype(jnp.float32)
    low = weights - high - middle
    kept = jnp.where(part == 0, high, jnp.where(part == 1, middle, jnp.where(part == 2, low, 0.0)))
    return kept.astype(jnp.bfloat16)


def iota(shape, dim):
    return lax.broadcasted_iota(jnp.int32, shape, dim)


def pack_kernel(block_ref, obs_ref, out_ref, raw, names_vmem, flat, rows, staged, sems):
    pairs = obs_ref.shape[1] // 2
    tiles = obs_ref.shape[2] // LANES
    fetches = [pltpu.make_async_copy(obs_ref.at[comp], raw.at[comp], sems.at[comp]) for comp in range(COMPS)]
    fetches.append(pltpu.make_async_copy(block_ref, names_vmem, sems.at[COMPS]))
    for fetch in fetches:
        fetch.start()
    some = pairs // 2
    height = some * PIECE
    leave = [
        pltpu.make_async_copy(
            staged.at[height * part : height * (part + 1)],
            out_ref.at[height * part : height * (part + 1)],
            sems.at[COMPS + 1 + part],
        )
        for part in range(2)
    ]
    for part in range(2):
        for comp in range(COMPS):
            if part == 0:
                fetches[comp].wait()
            for tile in range(tiles):
                at = ((part * COMPS + comp) * tiles + tile) * 2 * some
                own = slice(2 * some * part, 2 * some * (part + 1))
                flat[at : at + 2 * some, :] = raw[comp, own, tile * LANES : (tile + 1) * LANES].astype(jnp.float32)
                for rank in range(2):
                    values = flat[pl.ds(at + rank, some, stride=2), :]
                    to = height * part + (comp * 2 + rank) * tiles + tile
                    rows[pl.ds(to, some, stride=PIECE), :] = values
        if part == 0:
            fetches[COMPS].wait()
            column = as_column(names_vmem[...].astype(jnp.float32))
            hits = jnp.where(iota((pairs, LANES), 1).astype(jnp.float32) == column, 1.0, 0.0)
            histogram = jnp.broadcast_to(jnp.sum(hits, axis=0, keepdims=True), (some, LANES))
        rows[pl.ds(height * part + PIECE - 2, some, stride=PIECE), :] = histogram
        rows[pl.ds(height * part + PIECE - 1, some, stride=PIECE), :] = jnp.zeros((some, LANES), jnp.float32)
        own = slice(height * part, height * (part + 1))
        staged[own, :] = rows[own, :].astype(jnp.bfloat16)
        leave[part].start()
    for copy in leave:
        copy.wait()


def as_column(row):
    square = (row.shape[1], row.shape[1])
    own = jnp.where(iota(square, 0) == iota(square, 1), jnp.broadcast_to(row, square), 0.0)
    return jnp.sum(own, axis=1, keepdims=True)


def as_row(column):
    tall = (column.shape[0], LANES)
    own = jnp.where(iota(tall, 0) == iota(tall, 1) % column.shape[0], jnp.broadcast_to(column, tall), 0.0)
    return jnp.sum(own, axis=0, keepdims=True)


def synth_kernel(
    element_ref, coords_ref, block_ref, start_ref, end_ref, traces_ref,
    syn_ref, taper_ref, square_ref, spread_ref, columns_ref, places_ref,
    element_vmem, coords_vmem, block_vmem, start_vmem, end_vmem, start_smem, traces, wide, moved, sems,
):
    elements = traces_ref.shape[0]
    stations = syn_ref.shape[1]
    window = syn_ref.shape[2]
    tiles = window // LANES
    all_tiles = traces_ref.shape[3] // LANES
    step = SUBLANES * stations
    pairs = [
        (element_ref, element_vmem), (coords_ref, coords_vmem), (block_ref, block_vmem),
        (start_ref, start_vmem), (end_ref, end_vmem), (start_ref, start_smem),
    ]
    small = [pltpu.make_async_copy(a, b, sems.at[at]) for at, (a, b) in enumerate(pairs)]
    large = [
        pltpu.make_async_copy(traces_ref.at[:, comp], traces.at[comp], sems.at[len(pairs) + comp])
        for comp in range(COMPS)
    ]
    for fetch in small + large:
        fetch.start()
    for fetch in small:
        fetch.wait()

    span_row = (end_vmem[...] - start_vmem[...]).astype(jnp.float32)
    name_row = block_vmem[...].astype(jnp.float32)
    xi = as_column(coords_vmem[0:1, :])
    eta = as_column(coords_vmem[1:2, :])
    element = as_column(element_vmem[...].astype(jnp.float32))
    span = as_column(span_row)
    name = as_column(name_row)
    square = (stations, stations)
    twin = (jnp.broadcast_to(name_row, square) == name) & (iota(square, 1) < iota(square, 0))
    rank = jnp.sum(jnp.where(twin, 1.0, 0.0), axis=1, keepdims=True)
    first_row = (float(PIECE) * name + float(tiles) * rank).astype(jnp.int32)
    places_ref[...] = jnp.broadcast_to(first_row, places_ref.shape)
    columns_ref[...] = choose(iota((stations, LANES), 1), [span, name])

    for tile in range(tiles):
        lanes = slice(tile * LANES, (tile + 1) * LANES)
        sample = iota((stations, LANES), 1).astype(jnp.float32) + float(tile * LANES)
        inside = sample < span
        angle = jnp.where(inside, math.pi * (sample + 1.0) / (span + 1.0), 0.0)
        first = math.sqrt(2.0) * jnp.sin(angle)
        twice = 2.0 * jnp.cos(angle)
        tapers = [jnp.where(inside, first, 0.0)]
        tapers.append(twice * tapers[0])
        for _ in range(2, TAPERS):
            tapers.append(twice * tapers[-1] - tapers[-2])
        squares = tapers[0] * tapers[0]
        taper_ref[0, :, lanes] = tapers[0]
        for order in range(1, TAPERS):
            taper_ref[order, :, lanes] = tapers[order]
            squares = squares + tapers[order] * tapers[order]
        square_ref[:, lanes] = float(NF) * squares

    height = elements * FACE_PAD
    face = iota((FACE_PAD, LANES), 0)
    along_xi = choose(face // 5, lagrange_values(as_row(xi)))
    along_eta = choose(face % 5, lagrange_values(as_row(eta)))
    weights = jnp.where(face < FACE, along_xi * along_eta, 0.0)
    thirds = third_part(weights, iota((FACE_PAD, LANES), 1) // stations).astype(jnp.float32)
    element_row = as_row(element)
    for at in range(elements):
        spread_ref[at * FACE_PAD : (at + 1) * FACE_PAD, :] = jnp.where(element_row == at, thirds, 0.0).astype(jnp.bfloat16)

    face = iota((stations, FACE_PAD), 1)
    along_xi = choose(face // 5, lagrange_values(xi))
    along_eta = choose(face % 5, lagrange_values(eta))
    weights = jnp.where(face < FACE, along_xi * along_eta, 0.0)
    by_station = [third_part(weights, part).astype(jnp.float32) for part in range(3)]
    by_station = jnp.concatenate(by_station, axis=0)
    elements_3 = jnp.concatenate([element, element, element], axis=0)
    here = [jnp.where(elements_3 == at, by_station, 0.0).astype(jnp.bfloat16)[:, :FACE] for at in range(elements)]

    for comp in range(COMPS):
        large[comp].wait()
        total = None
        for at in range(elements):
            term = jnp.dot(here[at], traces[comp, at], preferred_element_type=jnp.float32)
            total = term if total is None else total + term
        sampled = total[:stations] + total[stations : 2 * stations] + total[2 * stations : 3 * stations]
        for tile in range(all_tiles):
            wide[pl.ds(tile * step + comp, stations, stride=SUBLANES), :] = sampled[
                :, tile * LANES : (tile + 1) * LANES
            ]
    wide[all_tiles * step :, :] = jnp.zeros((step, LANES), jnp.float32)

    lane = iota((SUBLANES, LANES), 1)

    def cut(station, carry):
        start = start_smem[0, station]
        first = start // LANES
        shift = start % LANES
        back = (LANES - shift) % LANES
        keep = lane < LANES - shift
        turned = []
        for tile in range(tiles + 1):
            at = pl.multiple_of((first + tile) * step + station * SUBLANES, SUBLANES)
            turned.append(pltpu.roll(wide[pl.ds(at, SUBLANES), :], back, 1))
        for tile in range(tiles):
            at = pl.multiple_of(tile * step + station * SUBLANES, SUBLANES)
            moved[pl.ds(at, SUBLANES), :] = jnp.where(keep, turned[tile], turned[tile + 1])
        return carry

    lax.fori_loop(0, stations, cut, 0, unroll=UNROLL)

    for comp in range(COMPS):
        for tile in range(tiles):
            piece = moved[pl.ds(tile * step + comp, stations, stride=SUBLANES), :]
            syn_ref[comp, :, tile * LANES : (tile + 1) * LANES] = piece.astype(jnp.bfloat16).astype(jnp.float32)


def misfit_kernel(
    scale, place_ref, columns_ref, taken_ref, syn_ref, taper_ref, square_ref,
    partial_ref, residual_ref, other_ref, factor_ref, rows, picked, sums,
):
    stations = columns_ref.shape[0]
    pairs = taken_ref.shape[0] // PIECE
    window = syn_ref.shape[2]
    tiles = window // LANES
    columns = columns_ref[...]
    rows[: taken_ref.shape[0], :] = taken_ref[...].astype(jnp.float32)
    for station in range(stations):
        place = place_ref[station : station + 1, 0:1][0, 0]
        for comp in range(COMPS):
            at = (comp * stations + station) * tiles
            picked[at : at + tiles, :] = rows[pl.ds(place + 2 * tiles * comp, tiles), :]
    counts = jnp.sum(rows[pl.ds(PIECE - 2, pairs, stride=PIECE), :], axis=0, keepdims=True)
    name = columns[:, 1:2]
    lane_f = iota((stations, LANES), 1).astype(jnp.float32)
    count = jnp.sum(jnp.where(lane_f == name, counts, 0.0), axis=1, keepdims=True)

    lane = iota((SUBLANES, LANES), 1).astype(jnp.float32)
    energies, powers = [], []
    for group in range(stations // SUBLANES):
        own = slice(group * SUBLANES, (group + 1) * SUBLANES)
        span = columns[own, 0:1]
        energy = jnp.zeros((SUBLANES, LANES), jnp.float32)
        power = jnp.zeros((SUBLANES, LANES), jnp.float32)
        parts = [jnp.zeros((SUBLANES, LANES), jnp.float32) for _ in range(TAPERS * COMPS)]
        for tile in range(tiles):
            lanes = slice(tile * LANES, (tile + 1) * LANES)
            inside = lane + float(tile * LANES) < span
            observed, residual = [], []
            for comp in range(COMPS):
                at = (comp * stations + group * SUBLANES) * tiles + tile
                observed.append(picked[pl.ds(at, SUBLANES, stride=tiles), :])
                residual.append(syn_ref[comp, own, lanes] - observed[comp])
                residual_ref[comp, own, lanes] = residual[comp]
            squares = observed[0] * observed[0] + observed[1] * observed[1] + observed[2] * observed[2]
            energy = energy + jnp.where(inside, squares, 0.0)
            squares = residual[0] * residual[0] + residual[1] * residual[1] + residual[2] * residual[2]
            power = power + square_ref[own, lanes] * squares
            for order in range(TAPERS):
                taper = taper_ref[order, own, lanes]
                for comp in range(COMPS):
                    at = order * COMPS + comp
                    parts[at] = parts[at] + taper * residual[comp]
        for at in range(TAPERS * COMPS):
            start = at * stations + group * SUBLANES
            sums[start : start + SUBLANES, :] = parts[at]
        energies.append(energy)
        powers.append(power)

    odd = (iota((2 * LANES, LANES), 0) + iota((2 * LANES, LANES), 1)) % 2
    odd = odd.astype(jnp.float32).astype(jnp.bfloat16)
    whole = sums[...]
    high = whole.astype(jnp.bfloat16)
    low = (whole - high.astype(jnp.float32)).astype(jnp.bfloat16)
    both = jnp.concatenate([high, low], axis=1)
    other = jnp.dot(both, odd, preferred_element_type=jnp.float32)
    other_ref[...] = other
    product = whole * other
    power = jnp.concatenate(powers, axis=0)
    for at in range(TAPERS * COMPS):
        power = power + product[at * stations : (at + 1) * stations]
    energy = jnp.sum(jnp.concatenate(energies, axis=0), axis=1, keepdims=True)
    power = jnp.sum(power, axis=1, keepdims=True)
    energy = energy / (3.0 * columns[:, 0:1]) + 1e-05
    weight = float(stations) / count
    factor = weight / (float(TAPERS * NF) * energy)
    factor_ref[...] = jnp.broadcast_to(factor, factor_ref.shape)
    partial = jnp.sum(scale * (factor * power), axis=0, keepdims=True)
    partial_ref[...] = jnp.broadcast_to(partial[:, :, None], partial_ref.shape)


def spread_kernel(
    start_ref, residual_ref, taper_ref, square_ref, other_ref, factor_ref, spread_ref,
    out_ref, start_smem, source, placed, staged, sems,
):
    fetch = pltpu.make_async_copy(start_ref, start_smem, sems.at[COMPS])
    fetch.start()
    elements = out_ref.shape[0]
    stations = factor_ref.shape[0]
    tiles = residual_ref.shape[2] // LANES
    all_tiles = out_ref.shape[3] // LANES
    step = SUBLANES * stations
    for comp in range(COMPS):
        for group in range(stations // SUBLANES):
            rows = slice(group * SUBLANES, (group + 1) * SUBLANES)
            factor = factor_ref[rows, :]
            for tile in range(tiles):
                lanes = slice(tile * LANES, (tile + 1) * LANES)
                value = square_ref[rows, lanes] * residual_ref[comp, rows, lanes]
                for order in range(TAPERS):
                    at = (order * COMPS + comp) * stations + group * SUBLANES
                    value = value + taper_ref[order, rows, lanes] * other_ref[at : at + SUBLANES, :]
                value = (factor * value).astype(jnp.bfloat16).astype(jnp.float32)
                at = tile * step + group * SUBLANES * SUBLANES + comp
                source[pl.ds(at, SUBLANES, stride=SUBLANES), :] = value

    placed[...] = jnp.zeros(placed.shape, jnp.float32)
    lane = iota((SUBLANES, LANES), 1)

    fetch.wait()

    def put(station, carry):
        start = start_smem[0, station]
        first = start // LANES
        shift = start % LANES
        keep = lane >= shift
        turned = [jnp.zeros((SUBLANES, LANES), jnp.float32)]
        for tile in range(tiles):
            at = pl.multiple_of(tile * step + station * SUBLANES, SUBLANES)
            turned.append(pltpu.roll(source[pl.ds(at, SUBLANES), :], shift, 1))
        turned.append(turned[0])
        for tile in range(tiles + 1):
            at = pl.multiple_of((first + tile) * step + station * SUBLANES, SUBLANES)
            placed[pl.ds(at, SUBLANES), :] = jnp.where(keep, turned[tile + 1], turned[tile])
        return carry

    lax.fori_loop(0, stations, put, 0, unroll=UNROLL)

    weights = spread_ref[:, : 3 * stations]
    for comp in range(COMPS):
        pieces = []
        for tile in range(all_tiles):
            piece = placed[pl.ds(tile * step + comp, stations, stride=SUBLANES), :]
            pieces.append(piece.astype(jnp.bfloat16))
        values = jnp.concatenate(pieces, axis=1)
        values = jnp.concatenate([values, values, values], axis=0)
        result = jnp.dot(weights, values, preferred_element_type=jnp.float32)
        for at in range(elements):
            rows = slice(at * FACE_PAD, at * FACE_PAD + FACE)
            staged[comp, at, :, :] = result[rows].astype(staged.dtype)
        pltpu.make_async_copy(staged.at[comp], out_ref.at[:, comp], sems.at[comp]).start()
    for comp in range(COMPS):
        pltpu.make_async_copy(staged.at[comp], out_ref.at[:, comp], sems.at[comp]).wait()


def whole(space=pltpu.VMEM):
    return pl.BlockSpec(memory_space=space)


def in_hbm(array):
    return pltpu.with_memory_space_constraint(array, pltpu.HBM)


def local(point_traces, rec_element, rec_coords, slot_block, window_start, window_end, obs_windows):
    slices = lax.axis_size("cuts")
    stations = rec_element.shape[0]
    window = obs_windows.shape[2]
    tiles = window // LANES
    samples = point_traces.shape[3]
    elements = point_traces.shape[0]
    line = (1, stations)
    blocks = in_hbm(slot_block.reshape(line))
    starts = in_hbm(window_start.reshape(line))
    params = pltpu.CompilerParams(vmem_limit_bytes=VMEM_LIMIT)
    f32, i32, bf16 = jnp.float32, jnp.int32, jnp.bfloat16
    far = whole(pltpu.HBM)

    packed = pl.pallas_call(
        pack_kernel,
        out_shape=jax.ShapeDtypeStruct((slices * PIECE, LANES), bf16),
        in_specs=[far, far],
        out_specs=far,
        scratch_shapes=[
            pltpu.VMEM((COMPS, obs_windows.shape[0], window), bf16),
            pltpu.VMEM(line, i32),
            pltpu.VMEM((COMPS * tiles * obs_windows.shape[0] + SUBLANES, LANES), f32),
            pltpu.VMEM((slices * PIECE + LAST, LANES), f32),
            pltpu.VMEM((slices * PIECE, LANES), bf16),
            pltpu.SemaphoreType.DMA((COMPS + 3,)),
        ],
        compiler_params=params,
        cost_estimate=pl.CostEstimate(flops=0, bytes_accessed=1 << 20, transcendentals=0),
        name="pack_observed",
    )(blocks, in_hbm(jnp.transpose(obs_windows, (1, 0, 2))))
    packed = packed.reshape(slices, PIECE // 2, 2, LANES)
    taken = lax.all_to_all(packed, "cuts", split_axis=0, concat_axis=0, tiled=True)
    taken = taken.reshape(slices * PIECE, LANES)

    step = SUBLANES * stations
    synthetic, tapers, squares, spread_weights, columns, places = pl.pallas_call(
        synth_kernel,
        out_shape=(
            jax.ShapeDtypeStruct((COMPS, stations, window), f32),
            jax.ShapeDtypeStruct((TAPERS, stations, window), f32),
            jax.ShapeDtypeStruct((stations, window), f32),
            jax.ShapeDtypeStruct((elements * FACE_PAD, LANES), bf16),
            jax.ShapeDtypeStruct((stations, LANES), f32),
            jax.ShapeDtypeStruct((stations, LANES), i32),
        ),
        in_specs=[far] * 6,
        out_specs=(whole(),) * 6,
        scratch_shapes=[
            pltpu.VMEM(line, i32),
            pltpu.VMEM((2, stations), f32),
            pltpu.VMEM(line, i32),
            pltpu.VMEM(line, i32),
            pltpu.VMEM(line, i32),
            pltpu.SMEM(line, i32),
            pltpu.VMEM((COMPS, elements) + point_traces.shape[2:], bf16),
            pltpu.VMEM(((samples // LANES + 1) * step, LANES), f32),
            pltpu.VMEM((tiles * step + SUBLANES, LANES), f32),
            pltpu.SemaphoreType.DMA((6 + COMPS,)),
        ],
        compiler_params=params,
        cost_estimate=pl.CostEstimate(
            flops=2 * 96 * 32 * 18 * samples, bytes_accessed=4 << 20, transcendentals=2 * stations * window
        ),
        name="synthetics",
    )(
        in_hbm(rec_element.reshape(line)),
        in_hbm(rec_coords),
        blocks,
        starts,
        in_hbm(window_end.reshape(line)),
        in_hbm(point_traces),
    )

    partial, residual, other, factor = pl.pallas_call(
        functools.partial(misfit_kernel, 0.5 / (3.0 * window * stations * slices)),
        out_shape=(
            pltpu.VMEM((slices, 1, LANES), f32),
            jax.ShapeDtypeStruct((COMPS, stations, window), f32),
            jax.ShapeDtypeStruct((TAPERS * COMPS * stations, LANES), f32),
            jax.ShapeDtypeStruct((stations, LANES), f32),
        ),
        in_specs=[whole()] * 6,
        out_specs=(whole(),) * 4,
        scratch_shapes=[
            pltpu.VMEM((slices * PIECE + LAST, LANES), f32),
            pltpu.VMEM((COMPS * stations * tiles + SUBLANES, LANES), f32),
            pltpu.VMEM((TAPERS * COMPS * stations, LANES), f32),
        ],
        compiler_params=params,
        cost_estimate=pl.CostEstimate(flops=1 << 24, bytes_accessed=3 << 20, transcendentals=0),
        name="misfit",
    )(places, columns, taken, synthetic, tapers, squares)
    partials = lax.all_to_all(partial, "cuts", split_axis=0, concat_axis=0, tiled=True)

    adjoint_points = pl.pallas_call(
        spread_kernel,
        out_shape=jax.ShapeDtypeStruct(point_traces.shape, point_traces.dtype),
        in_specs=[far] + [whole()] * 6,
        out_specs=far,
        scratch_shapes=[
            pltpu.SMEM(line, i32),
            pltpu.VMEM((tiles * step + SUBLANES, LANES), f32),
            pltpu.VMEM(((samples // LANES + 1) * step, LANES), f32),
            pltpu.VMEM((COMPS, elements) + point_traces.shape[2:], bf16),
            pltpu.SemaphoreType.DMA((COMPS + 1,)),
        ],
        compiler_params=params,
        cost_estimate=pl.CostEstimate(
            flops=2 * 192 * 96 * 3 * samples, bytes_accessed=6 << 20, transcendentals=0
        ),
        name="spread_adjoint",
    )(starts, residual, tapers, squares, other, factor, spread_weights)

    total_misfit = jnp.sum(partials[:, 0, :1], axis=0)
    return (adjoint_points, total_misfit)


def solution(mesh):
    return jax.shard_map(
        local,
        mesh=mesh,
        in_specs=(
            P(("event", "cuts"), None, None, None),
            P(("event", "cuts")),
            P(None, ("event", "cuts")),
            P(("event", "cuts"), None),
            P(("event", "cuts")),
            P(("event", "cuts")),
            P(("event", "cuts"), None, None),
        ),
        out_specs=(P(("event", "cuts"), None, None, None), P("event")),
        check_vma=False,
    )
```

```python
import functools
import math

import jax
import jax.numpy as jnp
from jax import lax
from jax.experimental import pallas as pl
from jax.experimental.pallas import tpu as pltpu
from jax.sharding import PartitionSpec as P

TAPERS = 5
NF = 512
COMPS = 3
LANES = 128
SUBLANES = 8
FACE = 25
FACE_PAD = 32
PIECE = 50
LAST = 64
VMEM_LIMIT = 48 * 1024 * 1024
UNROLL = 8

gll_nodes = (-1.0, -0.6546536707079771, 0.0, 0.6546536707079771, 1.0)


def lagrange_values(coordinate):
    values = []
    for first_node in range(5):
        value = jnp.ones_like(coordinate)
        for other_node in range(5):
            if other_node != first_node:
                value = (
                    value
                    * (coordinate - gll_nodes[other_node])
                    / (gll_nodes[first_node] - gll_nodes[other_node])
                )
        values.append(value)
    return values


def choose(index, values):
    chosen = jnp.where(index == 0, values[0], 0.0)
    for at in range(1, len(values)):
        chosen = jnp.where(index == at, values[at], chosen)
    return chosen


def third_part(weights, part):
    high = weights.astype(jnp.bfloat16).astype(jnp.float32)
    middle = (weights - high).astype(jnp.bfloat16).astype(jnp.float32)
    low = weights - high - middle
    kept = jnp.where(part == 0, high, jnp.where(part == 1, middle, jnp.where(part == 2, low, 0.0)))
    return kept.astype(jnp.bfloat16)


def iota(shape, dim):
    return lax.broadcasted_iota(jnp.int32, shape, dim)


def pack_kernel(block_ref, obs_ref, out_ref, raw, names_vmem, flat, rows, staged, sems):
    pairs = obs_ref.shape[1] // 2
    tiles = obs_ref.shape[2] // LANES
    some = pairs // 2
    fetches = [
        pltpu.make_async_copy(
            obs_ref.at[comp, 2 * some * part : 2 * some * (part + 1)],
            raw.at[comp, 2 * some * part : 2 * some * (part + 1)],
            sems.at[COMPS * part + comp],
        )
        for part in range(2)
        for comp in range(COMPS)
    ]
    names = pltpu.make_async_copy(block_ref, names_vmem, sems.at[2 * COMPS])
    names.start()
    for fetch in fetches:
        fetch.start()
    height = some * PIECE
    leave = [
        pltpu.make_async_copy(
            staged.at[height * part : height * (part + 1)],
            out_ref.at[height * part : height * (part + 1)],
            sems.at[2 * COMPS + 1 + part],
        )
        for part in range(2)
    ]
    names.wait()
    column = as_column(names_vmem[...].astype(jnp.float32))
    hits = jnp.where(iota((pairs, LANES), 1).astype(jnp.float32) == column, 1.0, 0.0)
    histogram = jnp.broadcast_to(jnp.sum(hits, axis=0, keepdims=True), (pairs, LANES))
    rows[pl.ds(PIECE - 2, pairs, stride=PIECE), :] = histogram
    rows[pl.ds(PIECE - 1, pairs, stride=PIECE), :] = jnp.zeros((pairs, LANES), jnp.float32)
    for part in range(2):
        for comp in range(COMPS):
            fetches[COMPS * part + comp].wait()
            for tile in range(tiles):
                at = ((part * COMPS + comp) * tiles + tile) * 2 * some
                own = slice(2 * some * part, 2 * some * (part + 1))
                flat[at : at + 2 * some, :] = raw[comp, own, tile * LANES : (tile + 1) * LANES].astype(jnp.float32)
                for rank in range(2):
                    values = flat[pl.ds(at + rank, some, stride=2), :]
                    to = height * part + (comp * 2 + rank) * tiles + tile
                    rows[pl.ds(to, some, stride=PIECE), :] = values
        own = slice(height * part, height * (part + 1))
        staged[own, :] = rows[own, :].astype(jnp.bfloat16)
        leave[part].start()
    for copy in leave:
        copy.wait()


def as_column(row):
    square = (row.shape[1], row.shape[1])
    own = jnp.where(iota(square, 0) == iota(square, 1), jnp.broadcast_to(row, square), 0.0)
    return jnp.sum(own, axis=1, keepdims=True)


def as_row(column):
    tall = (column.shape[0], LANES)
    own = jnp.where(iota(tall, 0) == iota(tall, 1) % column.shape[0], jnp.broadcast_to(column, tall), 0.0)
    return jnp.sum(own, axis=0, keepdims=True)


def synth_kernel(
    element_ref, coords_ref, block_ref, start_ref, end_ref, traces_ref,
    syn_ref, taper_ref, square_ref, spread_ref, columns_ref, places_ref,
    element_vmem, coords_vmem, block_vmem, start_vmem, end_vmem, start_smem, traces, wide, moved, sems,
):
    elements = traces_ref.shape[0]
    stations = syn_ref.shape[1]
    window = syn_ref.shape[2]
    tiles = window // LANES
    all_tiles = traces_ref.shape[3] // LANES
    step = SUBLANES * stations
    pairs = [
        (element_ref, element_vmem), (coords_ref, coords_vmem), (block_ref, block_vmem),
        (start_ref, start_vmem), (end_ref, end_vmem), (start_ref, start_smem),
    ]
    small = [pltpu.make_async_copy(a, b, sems.at[at]) for at, (a, b) in enumerate(pairs)]
    large = [
        pltpu.make_async_copy(traces_ref.at[:, comp], traces.at[comp], sems.at[len(pairs) + comp])
        for comp in range(COMPS)
    ]
    for fetch in small + large:
        fetch.start()
    for fetch in small:
        fetch.wait()

    span_row = (end_vmem[...] - start_vmem[...]).astype(jnp.float32)
    name_row = block_vmem[...].astype(jnp.float32)
    xi = as_column(coords_vmem[0:1, :])
    eta = as_column(coords_vmem[1:2, :])
    element = as_column(element_vmem[...].astype(jnp.float32))
    span = as_column(span_row)
    name = as_column(name_row)
    square = (stations, stations)
    twin = (jnp.broadcast_to(name_row, square) == name) & (iota(square, 1) < iota(square, 0))
    rank = jnp.sum(jnp.where(twin, 1.0, 0.0), axis=1, keepdims=True)
    first_row = (float(PIECE) * name + float(tiles) * rank).astype(jnp.int32)
    places_ref[...] = jnp.broadcast_to(first_row, places_ref.shape)
    columns_ref[...] = choose(iota((stations, LANES), 1), [span, name])

    for tile in range(tiles):
        lanes = slice(tile * LANES, (tile + 1) * LANES)
        sample = iota((stations, LANES), 1).astype(jnp.float32) + float(tile * LANES)
        inside = sample < span
        angle = jnp.where(inside, math.pi * (sample + 1.0) / (span + 1.0), 0.0)
        first = math.sqrt(2.0) * jnp.sin(angle)
        twice = 2.0 * jnp.cos(angle)
        tapers = [jnp.where(inside, first, 0.0)]
        tapers.append(twice * tapers[0])
        for _ in range(2, TAPERS):
            tapers.append(twice * tapers[-1] - tapers[-2])
        squares = tapers[0] * tapers[0]
        taper_ref[0, :, lanes] = tapers[0]
        for order in range(1, TAPERS):
            taper_ref[order, :, lanes] = tapers[order]
            squares = squares + tapers[order] * tapers[order]
        square_ref[:, lanes] = float(NF) * squares

    height = elements * FACE_PAD
    face = iota((FACE_PAD, LANES), 0)
    along_xi = choose(face // 5, lagrange_values(as_row(xi)))
    along_eta = choose(face % 5, lagrange_values(as_row(eta)))
    weights = jnp.where(face < FACE, along_xi * along_eta, 0.0)
    thirds = third_part(weights, iota((FACE_PAD, LANES), 1) // stations).astype(jnp.float32)
    element_row = as_row(element)
    for at in range(elements):
        spread_ref[at * FACE_PAD : (at + 1) * FACE_PAD, :] = jnp.where(element_row == at, thirds, 0.0).astype(jnp.bfloat16)

    face = iota((stations, FACE_PAD), 1)
    along_xi = choose(face // 5, lagrange_values(xi))
    along_eta = choose(face % 5, lagrange_values(eta))
    weights = jnp.where(face < FACE, along_xi * along_eta, 0.0)
    by_station = [third_part(weights, part).astype(jnp.float32) for part in range(3)]
    by_station = jnp.concatenate(by_station, axis=0)
    elements_3 = jnp.concatenate([element, element, element], axis=0)
    here = [jnp.where(elements_3 == at, by_station, 0.0).astype(jnp.bfloat16)[:, :FACE] for at in range(elements)]

    for comp in range(COMPS):
        large[comp].wait()
        total = None
        for at in range(elements):
            term = jnp.dot(here[at], traces[comp, at], preferred_element_type=jnp.float32)
            total = term if total is None else total + term
        sampled = total[:stations] + total[stations : 2 * stations] + total[2 * stations : 3 * stations]
        for tile in range(all_tiles):
            wide[pl.ds(tile * step + comp, stations, stride=SUBLANES), :] = sampled[
                :, tile * LANES : (tile + 1) * LANES
            ]
    wide[all_tiles * step :, :] = jnp.zeros((step, LANES), jnp.float32)

    lane = iota((SUBLANES, LANES), 1)

    def cut(station, carry):
        start = start_smem[0, station]
        first = start // LANES
        shift = start % LANES
        back = (LANES - shift) % LANES
        keep = lane < LANES - shift
        turned = []
        for tile in range(tiles + 1):
            at = pl.multiple_of((first + tile) * step + station * SUBLANES, SUBLANES)
            turned.append(pltpu.roll(wide[pl.ds(at, SUBLANES), :], back, 1))
        for tile in range(tiles):
            at = pl.multiple_of(tile * step + station * SUBLANES, SUBLANES)
            moved[pl.ds(at, SUBLANES), :] = jnp.where(keep, turned[tile], turned[tile + 1])
        return carry

    lax.fori_loop(0, stations, cut, 0, unroll=UNROLL)

    for comp in range(COMPS):
        for tile in range(tiles):
            piece = moved[pl.ds(tile * step + comp, stations, stride=SUBLANES), :]
            syn_ref[comp, :, tile * LANES : (tile + 1) * LANES] = piece.astype(jnp.bfloat16).astype(jnp.float32)


def misfit_kernel(
    scale, place_ref, columns_ref, taken_ref, syn_ref, taper_ref, square_ref,
    partial_ref, residual_ref, other_ref, factor_ref, rows, picked,
):
    stations = columns_ref.shape[0]
    pairs = taken_ref.shape[0] // PIECE
    window = syn_ref.shape[2]
    tiles = window // LANES
    columns = columns_ref[...]
    rows[: taken_ref.shape[0], :] = taken_ref[...].astype(jnp.float32)
    for station in range(stations):
        place = place_ref[station : station + 1, 0:1][0, 0]
        for comp in range(COMPS):
            at = (comp * stations + station) * tiles
            picked[at : at + tiles, :] = rows[pl.ds(place + 2 * tiles * comp, tiles), :]
    counts = jnp.sum(rows[pl.ds(PIECE - 2, pairs, stride=PIECE), :], axis=0, keepdims=True)
    name = columns[:, 1:2]
    lane_f = iota((stations, LANES), 1).astype(jnp.float32)
    count = jnp.sum(jnp.where(lane_f == name, counts, 0.0), axis=1, keepdims=True)

    lane = iota((SUBLANES, LANES), 1).astype(jnp.float32)
    odd = (iota((2 * LANES, LANES), 0) + iota((2 * LANES, LANES), 1)) % 2
    odd = odd.astype(jnp.float32).astype(jnp.bfloat16)
    height = TAPERS * COMPS * SUBLANES
    energies, powers = [], []
    for group in range(stations // SUBLANES):
        own = slice(group * SUBLANES, (group + 1) * SUBLANES)
        span = columns[own, 0:1]
        energy = jnp.zeros((SUBLANES, LANES), jnp.float32)
        power = jnp.zeros((SUBLANES, LANES), jnp.float32)
        parts = [jnp.zeros((SUBLANES, LANES), jnp.float32) for _ in range(TAPERS * COMPS)]
        for tile in range(tiles):
            lanes = slice(tile * LANES, (tile + 1) * LANES)
            inside = lane + float(tile * LANES) < span
            observed, residual = [], []
            for comp in range(COMPS):
                at = (comp * stations + group * SUBLANES) * tiles + tile
                observed.append(picked[pl.ds(at, SUBLANES, stride=tiles), :])
                residual.append(syn_ref[comp, own, lanes] - observed[comp])
                residual_ref[comp, own, lanes] = residual[comp]
            squares = observed[0] * observed[0] + observed[1] * observed[1] + observed[2] * observed[2]
            energy = energy + jnp.where(inside, squares, 0.0)
            squares = residual[0] * residual[0] + residual[1] * residual[1] + residual[2] * residual[2]
            power = power + square_ref[own, lanes] * squares
            for order in range(TAPERS):
                taper = taper_ref[order, own, lanes]
                for comp in range(COMPS):
                    at = order * COMPS + comp
                    parts[at] = parts[at] + taper * residual[comp]
        whole = jnp.concatenate(parts, axis=0)
        high = whole.astype(jnp.bfloat16)
        low = (whole - high.astype(jnp.float32)).astype(jnp.bfloat16)
        both = jnp.concatenate([high, low], axis=1)
        other = jnp.dot(both, odd, preferred_element_type=jnp.float32)
        other_ref[group * height : (group + 1) * height, :] = other
        product = whole * other
        for at in range(TAPERS * COMPS):
            power = power + product[at * SUBLANES : (at + 1) * SUBLANES]
        energies.append(energy)
        powers.append(power)

    power = jnp.concatenate(powers, axis=0)
    energy = jnp.sum(jnp.concatenate(energies, axis=0), axis=1, keepdims=True)
    power = jnp.sum(power, axis=1, keepdims=True)
    energy = energy / (3.0 * columns[:, 0:1]) + 1e-05
    weight = float(stations) / count
    factor = weight / (float(TAPERS * NF) * energy)
    factor_ref[...] = jnp.broadcast_to(factor, factor_ref.shape)
    partial = jnp.sum(scale * (factor * power), axis=0, keepdims=True)
    partial_ref[...] = jnp.broadcast_to(partial[:, :, None], partial_ref.shape)


def spread_kernel(
    start_ref, residual_ref, taper_ref, square_ref, other_ref, factor_ref, spread_ref,
    out_ref, start_smem, source, placed, staged, sems,
):
    fetch = pltpu.make_async_copy(start_ref, start_smem, sems.at[COMPS])
    fetch.start()
    elements = out_ref.shape[0]
    stations = factor_ref.shape[0]
    tiles = residual_ref.shape[2] // LANES
    all_tiles = out_ref.shape[3] // LANES
    step = SUBLANES * stations
    for comp in range(COMPS):
        for group in range(stations // SUBLANES):
            rows = slice(group * SUBLANES, (group + 1) * SUBLANES)
            factor = factor_ref[rows, :]
            for tile in range(tiles):
                lanes = slice(tile * LANES, (tile + 1) * LANES)
                value = square_ref[rows, lanes] * residual_ref[comp, rows, lanes]
                for order in range(TAPERS):
                    at = ((group * TAPERS + order) * COMPS + comp) * SUBLANES
                    value = value + taper_ref[order, rows, lanes] * other_ref[at : at + SUBLANES, :]
                value = (factor * value).astype(jnp.bfloat16).astype(jnp.float32)
                at = tile * step + group * SUBLANES * SUBLANES + comp
                source[pl.ds(at, SUBLANES, stride=SUBLANES), :] = value

    placed[...] = jnp.zeros(placed.shape, jnp.float32)
    lane = iota((SUBLANES, LANES), 1)

    fetch.wait()

    def put(station, carry):
        start = start_smem[0, station]
        first = start // LANES
        shift = start % LANES
        keep = lane >= shift
        turned = [jnp.zeros((SUBLANES, LANES), jnp.float32)]
        for tile in range(tiles):
            at = pl.multiple_of(tile * step + station * SUBLANES, SUBLANES)
            turned.append(pltpu.roll(source[pl.ds(at, SUBLANES), :], shift, 1))
        turned.append(turned[0])
        for tile in range(tiles + 1):
            at = pl.multiple_of((first + tile) * step + station * SUBLANES, SUBLANES)
            placed[pl.ds(at, SUBLANES), :] = jnp.where(keep, turned[tile + 1], turned[tile])
        return carry

    lax.fori_loop(0, stations, put, 0, unroll=UNROLL)

    weights = spread_ref[:, : 3 * stations]
    for comp in range(COMPS):
        pieces = []
        for tile in range(all_tiles):
            piece = placed[pl.ds(tile * step + comp, stations, stride=SUBLANES), :]
            pieces.append(piece.astype(jnp.bfloat16))
        values = jnp.concatenate(pieces, axis=1)
        values = jnp.concatenate([values, values, values], axis=0)
        result = jnp.dot(weights, values, preferred_element_type=jnp.float32)
        for at in range(elements):
            rows = slice(at * FACE_PAD, at * FACE_PAD + FACE)
            staged[comp, at, :, :] = result[rows].astype(staged.dtype)
        pltpu.make_async_copy(staged.at[comp], out_ref.at[:, comp], sems.at[comp]).start()
    for comp in range(COMPS):
        pltpu.make_async_copy(staged.at[comp], out_ref.at[:, comp], sems.at[comp]).wait()


def whole(space=pltpu.VMEM):
    return pl.BlockSpec(memory_space=space)


def in_hbm(array):
    return pltpu.with_memory_space_constraint(array, pltpu.HBM)


def local(point_traces, rec_element, rec_coords, slot_block, window_start, window_end, obs_windows):
    slices = lax.axis_size("cuts")
    stations = rec_element.shape[0]
    window = obs_windows.shape[2]
    tiles = window // LANES
    samples = point_traces.shape[3]
    elements = point_traces.shape[0]
    line = (1, stations)
    blocks = in_hbm(slot_block.reshape(line))
    starts = in_hbm(window_start.reshape(line))
    params = pltpu.CompilerParams(vmem_limit_bytes=VMEM_LIMIT)
    f32, i32, bf16 = jnp.float32, jnp.int32, jnp.bfloat16
    far = whole(pltpu.HBM)

    packed = pl.pallas_call(
        pack_kernel,
        out_shape=jax.ShapeDtypeStruct((slices * PIECE, LANES), bf16),
        in_specs=[far, far],
        out_specs=far,
        scratch_shapes=[
            pltpu.VMEM((COMPS, obs_windows.shape[0], window), bf16),
            pltpu.VMEM(line, i32),
            pltpu.VMEM((COMPS * tiles * obs_windows.shape[0] + SUBLANES, LANES), f32),
            pltpu.VMEM((slices * PIECE + LAST, LANES), f32),
            pltpu.VMEM((slices * PIECE, LANES), bf16),
            pltpu.SemaphoreType.DMA((2 * COMPS + 3,)),
        ],
        compiler_params=params,
        cost_estimate=pl.CostEstimate(flops=0, bytes_accessed=1 << 20, transcendentals=0),
        name="pack_observed",
    )(blocks, in_hbm(jnp.transpose(obs_windows, (1, 0, 2))))
    packed = packed.reshape(slices, PIECE // 2, 2, LANES)
    taken = lax.all_to_all(packed, "cuts", split_axis=0, concat_axis=0, tiled=True)
    taken = taken.reshape(slices * PIECE, LANES)

    step = SUBLANES * stations
    synthetic, tapers, squares, spread_weights, columns, places = pl.pallas_call(
        synth_kernel,
        out_shape=(
            jax.ShapeDtypeStruct((COMPS, stations, window), f32),
            jax.ShapeDtypeStruct((TAPERS, stations, window), f32),
            jax.ShapeDtypeStruct((stations, window), f32),
            jax.ShapeDtypeStruct((elements * FACE_PAD, LANES), bf16),
            jax.ShapeDtypeStruct((stations, LANES), f32),
            jax.ShapeDtypeStruct((stations, LANES), i32),
        ),
        in_specs=[far] * 6,
        out_specs=(whole(),) * 6,
        scratch_shapes=[
            pltpu.VMEM(line, i32),
            pltpu.VMEM((2, stations), f32),
            pltpu.VMEM(line, i32),
            pltpu.VMEM(line, i32),
            pltpu.VMEM(line, i32),
            pltpu.SMEM(line, i32),
            pltpu.VMEM((COMPS, elements) + point_traces.shape[2:], bf16),
            pltpu.VMEM(((samples // LANES + 1) * step, LANES), f32),
            pltpu.VMEM((tiles * step + SUBLANES, LANES), f32),
            pltpu.SemaphoreType.DMA((6 + COMPS,)),
        ],
        compiler_params=params,
        cost_estimate=pl.CostEstimate(
            flops=2 * 96 * 32 * 18 * samples, bytes_accessed=4 << 20, transcendentals=2 * stations * window
        ),
        name="synthetics",
    )(
        in_hbm(rec_element.reshape(line)),
        in_hbm(rec_coords),
        blocks,
        starts,
        in_hbm(window_end.reshape(line)),
        in_hbm(point_traces),
    )

    partial, residual, other, factor = pl.pallas_call(
        functools.partial(misfit_kernel, 0.5 / (3.0 * window * stations * slices)),
        out_shape=(
            pltpu.VMEM((slices, 1, LANES), f32),
            jax.ShapeDtypeStruct((COMPS, stations, window), f32),
            jax.ShapeDtypeStruct((TAPERS * COMPS * stations, LANES), f32),
            jax.ShapeDtypeStruct((stations, LANES), f32),
        ),
        in_specs=[whole()] * 6,
        out_specs=(whole(),) * 4,
        scratch_shapes=[
            pltpu.VMEM((slices * PIECE + LAST, LANES), f32),
            pltpu.VMEM((COMPS * stations * tiles + SUBLANES, LANES), f32),
        ],
        compiler_params=params,
        cost_estimate=pl.CostEstimate(flops=1 << 24, bytes_accessed=3 << 20, transcendentals=0),
        name="misfit",
    )(places, columns, taken, synthetic, tapers, squares)
    partials = lax.all_to_all(partial, "cuts", split_axis=0, concat_axis=0, tiled=True)

    adjoint_points = pl.pallas_call(
        spread_kernel,
        out_shape=jax.ShapeDtypeStruct(point_traces.shape, point_traces.dtype),
        in_specs=[far] + [whole()] * 6,
        out_specs=far,
        scratch_shapes=[
            pltpu.SMEM(line, i32),
            pltpu.VMEM((tiles * step + SUBLANES, LANES), f32),
            pltpu.VMEM(((samples // LANES + 1) * step, LANES), f32),
            pltpu.VMEM((COMPS, elements) + point_traces.shape[2:], bf16),
            pltpu.SemaphoreType.DMA((COMPS + 1,)),
        ],
        compiler_params=params,
        cost_estimate=pl.CostEstimate(
            flops=2 * 192 * 96 * 3 * samples, bytes_accessed=6 << 20, transcendentals=0
        ),
        name="spread_adjoint",
    )(starts, residual, tapers, squares, other, factor, spread_weights)

    total_misfit = jnp.sum(partials[:, 0, :1], axis=0)
    return (adjoint_points, total_misfit)


def solution(mesh):
    return jax.shard_map(
        local,
        mesh=mesh,
        in_specs=(
            P(("event", "cuts"), None, None, None),
            P(("event", "cuts")),
            P(None, ("event", "cuts")),
            P(("event", "cuts"), None),
            P(("event", "cuts")),
            P(("event", "cuts")),
            P(("event", "cuts"), None, None),
        ),
        out_specs=(P(("event", "cuts"), None, None, None), P("event")),
        check_vma=False,
    )
```

```python
import functools
import math

import jax
import jax.numpy as jnp
from jax import lax
from jax.experimental import pallas as pl
from jax.experimental.pallas import tpu as pltpu
from jax.sharding import PartitionSpec as P

TAPERS = 5
NF = 512
COMPS = 3
LANES = 128
SUBLANES = 8
FACE = 25
FACE_PAD = 32
PIECE = 50
PARTS = 4
LAST = 64
VMEM_LIMIT = 48 * 1024 * 1024
UNROLL = 8

gll_nodes = (-1.0, -0.6546536707079771, 0.0, 0.6546536707079771, 1.0)


def lagrange_values(coordinate):
    values = []
    for first_node in range(5):
        value = jnp.ones_like(coordinate)
        for other_node in range(5):
            if other_node != first_node:
                value = (
                    value
                    * (coordinate - gll_nodes[other_node])
                    / (gll_nodes[first_node] - gll_nodes[other_node])
                )
        values.append(value)
    return values


def choose(index, values):
    chosen = jnp.where(index == 0, values[0], 0.0)
    for at in range(1, len(values)):
        chosen = jnp.where(index == at, values[at], chosen)
    return chosen


def third_part(weights, part):
    high = weights.astype(jnp.bfloat16).astype(jnp.float32)
    middle = (weights - high).astype(jnp.bfloat16).astype(jnp.float32)
    low = weights - high - middle
    kept = jnp.where(part == 0, high, jnp.where(part == 1, middle, jnp.where(part == 2, low, 0.0)))
    return kept.astype(jnp.bfloat16)


def iota(shape, dim):
    return lax.broadcasted_iota(jnp.int32, shape, dim)


def pack_kernel(block_ref, obs_ref, out_ref, raw, names_vmem, flat, rows, staged, sems):
    pairs = obs_ref.shape[1] // 2
    tiles = obs_ref.shape[2] // LANES
    some = pairs // PARTS
    fetches = [
        pltpu.make_async_copy(
            obs_ref.at[comp, 2 * some * part : 2 * some * (part + 1)],
            raw.at[comp, 2 * some * part : 2 * some * (part + 1)],
            sems.at[COMPS * part + comp],
        )
        for part in range(PARTS)
        for comp in range(COMPS)
    ]
    names = pltpu.make_async_copy(block_ref, names_vmem, sems.at[PARTS * COMPS])
    names.start()
    for fetch in fetches:
        fetch.start()
    height = some * PIECE
    leave = [
        pltpu.make_async_copy(
            staged.at[height * part : height * (part + 1)],
            out_ref.at[height * part : height * (part + 1)],
            sems.at[PARTS * COMPS + 1 + part],
        )
        for part in range(PARTS)
    ]
    names.wait()
    column = as_column(names_vmem[...].astype(jnp.float32))
    hits = jnp.where(iota((pairs, LANES), 1).astype(jnp.float32) == column, 1.0, 0.0)
    histogram = jnp.broadcast_to(jnp.sum(hits, axis=0, keepdims=True), (pairs, LANES))
    rows[pl.ds(PIECE - 2, pairs, stride=PIECE), :] = histogram
    rows[pl.ds(PIECE - 1, pairs, stride=PIECE), :] = jnp.zeros((pairs, LANES), jnp.float32)
    for part in range(PARTS):
        for comp in range(COMPS):
            fetches[COMPS * part + comp].wait()
            for tile in range(tiles):
                at = ((part * COMPS + comp) * tiles + tile) * 2 * some
                own = slice(2 * some * part, 2 * some * (part + 1))
                flat[at : at + 2 * some, :] = raw[comp, own, tile * LANES : (tile + 1) * LANES].astype(jnp.float32)
                for rank in range(2):
                    values = flat[pl.ds(at + rank, some, stride=2), :]
                    to = height * part + (comp * 2 + rank) * tiles + tile
                    rows[pl.ds(to, some, stride=PIECE), :] = values
        own = slice(height * part, height * (part + 1))
        staged[own, :] = rows[own, :].astype(jnp.bfloat16)
        leave[part].start()
    for copy in leave:
        copy.wait()


def as_column(row):
    square = (row.shape[1], row.shape[1])
    own = jnp.where(iota(square, 0) == iota(square, 1), jnp.broadcast_to(row, square), 0.0)
    return jnp.sum(own, axis=1, keepdims=True)


def as_row(column):
    tall = (column.shape[0], LANES)
    own = jnp.where(iota(tall, 0) == iota(tall, 1) % column.shape[0], jnp.broadcast_to(column, tall), 0.0)
    return jnp.sum(own, axis=0, keepdims=True)


def synth_kernel(
    element_ref, coords_ref, block_ref, start_ref, end_ref, traces_ref,
    syn_ref, taper_ref, square_ref, spread_ref, columns_ref, places_ref,
    element_vmem, coords_vmem, block_vmem, start_vmem, end_vmem, start_smem, traces, wide, moved, sems,
):
    elements = traces_ref.shape[0]
    stations = syn_ref.shape[1]
    window = syn_ref.shape[2]
    tiles = window // LANES
    all_tiles = traces_ref.shape[3] // LANES
    step = SUBLANES * stations
    pairs = [
        (element_ref, element_vmem), (coords_ref, coords_vmem), (block_ref, block_vmem),
        (start_ref, start_vmem), (end_ref, end_vmem), (start_ref, start_smem),
    ]
    small = [pltpu.make_async_copy(a, b, sems.at[at]) for at, (a, b) in enumerate(pairs)]
    large = [
        pltpu.make_async_copy(traces_ref.at[:, comp], traces.at[comp], sems.at[len(pairs) + comp])
        for comp in range(COMPS)
    ]
    for fetch in small + large:
        fetch.start()
    for fetch in small:
        fetch.wait()

    span_row = (end_vmem[...] - start_vmem[...]).astype(jnp.float32)
    name_row = block_vmem[...].astype(jnp.float32)
    xi = as_column(coords_vmem[0:1, :])
    eta = as_column(coords_vmem[1:2, :])
    element = as_column(element_vmem[...].astype(jnp.float32))
    span = as_column(span_row)
    name = as_column(name_row)
    square = (stations, stations)
    twin = (jnp.broadcast_to(name_row, square) == name) & (iota(square, 1) < iota(square, 0))
    rank = jnp.sum(jnp.where(twin, 1.0, 0.0), axis=1, keepdims=True)
    first_row = (float(PIECE) * name + float(tiles) * rank).astype(jnp.int32)
    places_ref[...] = jnp.broadcast_to(first_row, places_ref.shape)
    columns_ref[...] = choose(iota((stations, LANES), 1), [span, name])

    for tile in range(tiles):
        lanes = slice(tile * LANES, (tile + 1) * LANES)
        sample = iota((stations, LANES), 1).astype(jnp.float32) + float(tile * LANES)
        inside = sample < span
        angle = jnp.where(inside, math.pi * (sample + 1.0) / (span + 1.0), 0.0)
        first = math.sqrt(2.0) * jnp.sin(angle)
        twice = 2.0 * jnp.cos(angle)
        tapers = [jnp.where(inside, first, 0.0)]
        tapers.append(twice * tapers[0])
        for _ in range(2, TAPERS):
            tapers.append(twice * tapers[-1] - tapers[-2])
        squares = tapers[0] * tapers[0]
        taper_ref[0, :, lanes] = tapers[0]
        for order in range(1, TAPERS):
            taper_ref[order, :, lanes] = tapers[order]
            squares = squares + tapers[order] * tapers[order]
        square_ref[:, lanes] = float(NF) * squares

    height = elements * FACE_PAD
    face = iota((FACE_PAD, LANES), 0)
    along_xi = choose(face // 5, lagrange_values(as_row(xi)))
    along_eta = choose(face % 5, lagrange_values(as_row(eta)))
    weights = jnp.where(face < FACE, along_xi * along_eta, 0.0)
    thirds = third_part(weights, iota((FACE_PAD, LANES), 1) // stations).astype(jnp.float32)
    element_row = as_row(element)
    for at in range(elements):
        spread_ref[at * FACE_PAD : (at + 1) * FACE_PAD, :] = jnp.where(element_row == at, thirds, 0.0).astype(jnp.bfloat16)

    face = iota((stations, FACE_PAD), 1)
    along_xi = choose(face // 5, lagrange_values(xi))
    along_eta = choose(face % 5, lagrange_values(eta))
    weights = jnp.where(face < FACE, along_xi * along_eta, 0.0)
    by_station = [third_part(weights, part).astype(jnp.float32) for part in range(3)]
    by_station = jnp.concatenate(by_station, axis=0)
    elements_3 = jnp.concatenate([element, element, element], axis=0)
    here = [jnp.where(elements_3 == at, by_station, 0.0).astype(jnp.bfloat16)[:, :FACE] for at in range(elements)]

    for comp in range(COMPS):
        large[comp].wait()
        total = None
        for at in range(elements):
            term = jnp.dot(here[at], traces[comp, at], preferred_element_type=jnp.float32)
            total = term if total is None else total + term
        sampled = total[:stations] + total[stations : 2 * stations] + total[2 * stations : 3 * stations]
        for tile in range(all_tiles):
            wide[pl.ds(tile * step + comp, stations, stride=SUBLANES), :] = sampled[
                :, tile * LANES : (tile + 1) * LANES
            ]
    wide[all_tiles * step :, :] = jnp.zeros((step, LANES), jnp.float32)

    lane = iota((SUBLANES, LANES), 1)

    def cut(station, carry):
        start = start_smem[0, station]
        first = start // LANES
        shift = start % LANES
        back = (LANES - shift) % LANES
        keep = lane < LANES - shift
        turned = []
        for tile in range(tiles + 1):
            at = pl.multiple_of((first + tile) * step + station * SUBLANES, SUBLANES)
            turned.append(pltpu.roll(wide[pl.ds(at, SUBLANES), :], back, 1))
        for tile in range(tiles):
            at = pl.multiple_of(tile * step + station * SUBLANES, SUBLANES)
            moved[pl.ds(at, SUBLANES), :] = jnp.where(keep, turned[tile], turned[tile + 1])
        return carry

    lax.fori_loop(0, stations, cut, 0, unroll=UNROLL)

    for comp in range(COMPS):
        for tile in range(tiles):
            piece = moved[pl.ds(tile * step + comp, stations, stride=SUBLANES), :]
            syn_ref[comp, :, tile * LANES : (tile + 1) * LANES] = piece.astype(jnp.bfloat16).astype(jnp.float32)


def misfit_kernel(
    scale, place_ref, columns_ref, taken_ref, syn_ref, taper_ref, square_ref,
    partial_ref, residual_ref, other_ref, factor_ref, rows, picked,
):
    stations = columns_ref.shape[0]
    pairs = taken_ref.shape[0] // PIECE
    window = syn_ref.shape[2]
    tiles = window // LANES
    columns = columns_ref[...]
    rows[: taken_ref.shape[0], :] = taken_ref[...].astype(jnp.float32)
    for station in range(stations):
        place = place_ref[station : station + 1, 0:1][0, 0]
        for comp in range(COMPS):
            at = (comp * stations + station) * tiles
            picked[at : at + tiles, :] = rows[pl.ds(place + 2 * tiles * comp, tiles), :]
    counts = jnp.sum(rows[pl.ds(PIECE - 2, pairs, stride=PIECE), :], axis=0, keepdims=True)
    name = columns[:, 1:2]
    lane_f = iota((stations, LANES), 1).astype(jnp.float32)
    count = jnp.sum(jnp.where(lane_f == name, counts, 0.0), axis=1, keepdims=True)

    lane = iota((SUBLANES, LANES), 1).astype(jnp.float32)
    odd = (iota((2 * LANES, LANES), 0) + iota((2 * LANES, LANES), 1)) % 2
    odd = odd.astype(jnp.float32).astype(jnp.bfloat16)
    height = TAPERS * COMPS * SUBLANES
    energies, powers = [], []
    for group in range(stations // SUBLANES):
        own = slice(group * SUBLANES, (group + 1) * SUBLANES)
        span = columns[own, 0:1]
        energy = jnp.zeros((SUBLANES, LANES), jnp.float32)
        power = jnp.zeros((SUBLANES, LANES), jnp.float32)
        parts = [jnp.zeros((SUBLANES, LANES), jnp.float32) for _ in range(TAPERS * COMPS)]
        for tile in range(tiles):
            lanes = slice(tile * LANES, (tile + 1) * LANES)
            inside = lane + float(tile * LANES) < span
            observed, residual = [], []
            for comp in range(COMPS):
                at = (comp * stations + group * SUBLANES) * tiles + tile
                observed.append(picked[pl.ds(at, SUBLANES, stride=tiles), :])
                residual.append(syn_ref[comp, own, lanes] - observed[comp])
                residual_ref[comp, own, lanes] = residual[comp]
            squares = observed[0] * observed[0] + observed[1] * observed[1] + observed[2] * observed[2]
            energy = energy + jnp.where(inside, squares, 0.0)
            squares = residual[0] * residual[0] + residual[1] * residual[1] + residual[2] * residual[2]
            power = power + square_ref[own, lanes] * squares
            for order in range(TAPERS):
                taper = taper_ref[order, own, lanes]
                for comp in range(COMPS):
                    at = order * COMPS + comp
                    parts[at] = parts[at] + taper * residual[comp]
        whole = jnp.concatenate(parts, axis=0)
        high = whole.astype(jnp.bfloat16)
        low = (whole - high.astype(jnp.float32)).astype(jnp.bfloat16)
        both = jnp.concatenate([high, low], axis=1)
        other = jnp.dot(both, odd, preferred_element_type=jnp.float32)
        other_ref[group * height : (group + 1) * height, :] = other
        product = whole * other
        for at in range(TAPERS * COMPS):
            power = power + product[at * SUBLANES : (at + 1) * SUBLANES]
        energies.append(energy)
        powers.append(power)

    power = jnp.concatenate(powers, axis=0)
    energy = jnp.sum(jnp.concatenate(energies, axis=0), axis=1, keepdims=True)
    power = jnp.sum(power, axis=1, keepdims=True)
    energy = energy / (3.0 * columns[:, 0:1]) + 1e-05
    weight = float(stations) / count
    factor = weight / (float(TAPERS * NF) * energy)
    factor_ref[...] = jnp.broadcast_to(factor, factor_ref.shape)
    partial = jnp.sum(scale * (factor * power), axis=0, keepdims=True)
    partial_ref[...] = jnp.broadcast_to(partial[:, :, None], partial_ref.shape)


def spread_kernel(
    start_ref, residual_ref, taper_ref, square_ref, other_ref, factor_ref, spread_ref,
    out_ref, start_smem, source, placed, staged, sems,
):
    fetch = pltpu.make_async_copy(start_ref, start_smem, sems.at[COMPS])
    fetch.start()
    elements = out_ref.shape[0]
    stations = factor_ref.shape[0]
    tiles = residual_ref.shape[2] // LANES
    all_tiles = out_ref.shape[3] // LANES
    step = SUBLANES * stations
    for comp in range(COMPS):
        for group in range(stations // SUBLANES):
            rows = slice(group * SUBLANES, (group + 1) * SUBLANES)
            factor = factor_ref[rows, :]
            for tile in range(tiles):
                lanes = slice(tile * LANES, (tile + 1) * LANES)
                value = square_ref[rows, lanes] * residual_ref[comp, rows, lanes]
                for order in range(TAPERS):
                    at = ((group * TAPERS + order) * COMPS + comp) * SUBLANES
                    value = value + taper_ref[order, rows, lanes] * other_ref[at : at + SUBLANES, :]
                value = (factor * value).astype(jnp.bfloat16).astype(jnp.float32)
                at = tile * step + group * SUBLANES * SUBLANES + comp
                source[pl.ds(at, SUBLANES, stride=SUBLANES), :] = value

    placed[...] = jnp.zeros(placed.shape, jnp.float32)
    lane = iota((SUBLANES, LANES), 1)

    fetch.wait()

    def put(station, carry):
        start = start_smem[0, station]
        first = start // LANES
        shift = start % LANES
        keep = lane >= shift
        turned = [jnp.zeros((SUBLANES, LANES), jnp.float32)]
        for tile in range(tiles):
            at = pl.multiple_of(tile * step + station * SUBLANES, SUBLANES)
            turned.append(pltpu.roll(source[pl.ds(at, SUBLANES), :], shift, 1))
        turned.append(turned[0])
        for tile in range(tiles + 1):
            at = pl.multiple_of((first + tile) * step + station * SUBLANES, SUBLANES)
            placed[pl.ds(at, SUBLANES), :] = jnp.where(keep, turned[tile + 1], turned[tile])
        return carry

    lax.fori_loop(0, stations, put, 0, unroll=UNROLL)

    weights = spread_ref[:, : 3 * stations]
    for comp in range(COMPS):
        pieces = []
        for tile in range(all_tiles):
            piece = placed[pl.ds(tile * step + comp, stations, stride=SUBLANES), :]
            pieces.append(piece.astype(jnp.bfloat16))
        values = jnp.concatenate(pieces, axis=1)
        values = jnp.concatenate([values, values, values], axis=0)
        result = jnp.dot(weights, values, preferred_element_type=jnp.float32)
        for at in range(elements):
            rows = slice(at * FACE_PAD, at * FACE_PAD + FACE)
            staged[comp, at, :, :] = result[rows].astype(staged.dtype)
        pltpu.make_async_copy(staged.at[comp], out_ref.at[:, comp], sems.at[comp]).start()
    for comp in range(COMPS):
        pltpu.make_async_copy(staged.at[comp], out_ref.at[:, comp], sems.at[comp]).wait()


def whole(space=pltpu.VMEM):
    return pl.BlockSpec(memory_space=space)


def in_hbm(array):
    return pltpu.with_memory_space_constraint(array, pltpu.HBM)


def local(point_traces, rec_element, rec_coords, slot_block, window_start, window_end, obs_windows):
    slices = lax.axis_size("cuts")
    stations = rec_element.shape[0]
    window = obs_windows.shape[2]
    tiles = window // LANES
    samples = point_traces.shape[3]
    elements = point_traces.shape[0]
    line = (1, stations)
    blocks = in_hbm(slot_block.reshape(line))
    starts = in_hbm(window_start.reshape(line))
    params = pltpu.CompilerParams(vmem_limit_bytes=VMEM_LIMIT)
    f32, i32, bf16 = jnp.float32, jnp.int32, jnp.bfloat16
    far = whole(pltpu.HBM)

    packed = pl.pallas_call(
        pack_kernel,
        out_shape=jax.ShapeDtypeStruct((slices * PIECE, LANES), bf16),
        in_specs=[far, far],
        out_specs=far,
        scratch_shapes=[
            pltpu.VMEM((COMPS, obs_windows.shape[0], window), bf16),
            pltpu.VMEM(line, i32),
            pltpu.VMEM((COMPS * tiles * obs_windows.shape[0] + SUBLANES, LANES), f32),
            pltpu.VMEM((slices * PIECE + LAST, LANES), f32),
            pltpu.VMEM((slices * PIECE, LANES), bf16),
            pltpu.SemaphoreType.DMA((PARTS * (COMPS + 1) + 1,)),
        ],
        compiler_params=params,
        cost_estimate=pl.CostEstimate(flops=0, bytes_accessed=1 << 20, transcendentals=0),
        name="pack_observed",
    )(blocks, in_hbm(jnp.transpose(obs_windows, (1, 0, 2))))
    packed = packed.reshape(slices, PIECE // 2, 2, LANES)
    taken = lax.all_to_all(packed, "cuts", split_axis=0, concat_axis=0, tiled=True)
    taken = taken.reshape(slices * PIECE, LANES)

    step = SUBLANES * stations
    synthetic, tapers, squares, spread_weights, columns, places = pl.pallas_call(
        synth_kernel,
        out_shape=(
            jax.ShapeDtypeStruct((COMPS, stations, window), f32),
            jax.ShapeDtypeStruct((TAPERS, stations, window), f32),
            jax.ShapeDtypeStruct((stations, window), f32),
            jax.ShapeDtypeStruct((elements * FACE_PAD, LANES), bf16),
            jax.ShapeDtypeStruct((stations, LANES), f32),
            jax.ShapeDtypeStruct((stations, LANES), i32),
        ),
        in_specs=[far] * 6,
        out_specs=(whole(),) * 6,
        scratch_shapes=[
            pltpu.VMEM(line, i32),
            pltpu.VMEM((2, stations), f32),
            pltpu.VMEM(line, i32),
            pltpu.VMEM(line, i32),
            pltpu.VMEM(line, i32),
            pltpu.SMEM(line, i32),
            pltpu.VMEM((COMPS, elements) + point_traces.shape[2:], bf16),
            pltpu.VMEM(((samples // LANES + 1) * step, LANES), f32),
            pltpu.VMEM((tiles * step + SUBLANES, LANES), f32),
            pltpu.SemaphoreType.DMA((6 + COMPS,)),
        ],
        compiler_params=params,
        cost_estimate=pl.CostEstimate(
            flops=2 * 96 * 32 * 18 * samples, bytes_accessed=4 << 20, transcendentals=2 * stations * window
        ),
        name="synthetics",
    )(
        in_hbm(rec_element.reshape(line)),
        in_hbm(rec_coords),
        blocks,
        starts,
        in_hbm(window_end.reshape(line)),
        in_hbm(point_traces),
    )

    partial, residual, other, factor = pl.pallas_call(
        functools.partial(misfit_kernel, 0.5 / (3.0 * window * stations * slices)),
        out_shape=(
            pltpu.VMEM((slices, 1, LANES), f32),
            jax.ShapeDtypeStruct((COMPS, stations, window), f32),
            jax.ShapeDtypeStruct((TAPERS * COMPS * stations, LANES), f32),
            jax.ShapeDtypeStruct((stations, LANES), f32),
        ),
        in_specs=[whole()] * 6,
        out_specs=(whole(),) * 4,
        scratch_shapes=[
            pltpu.VMEM((slices * PIECE + LAST, LANES), f32),
            pltpu.VMEM((COMPS * stations * tiles + SUBLANES, LANES), f32),
        ],
        compiler_params=params,
        cost_estimate=pl.CostEstimate(flops=1 << 24, bytes_accessed=3 << 20, transcendentals=0),
        name="misfit",
    )(places, columns, taken, synthetic, tapers, squares)
    partials = lax.all_to_all(partial, "cuts", split_axis=0, concat_axis=0, tiled=True)

    adjoint_points = pl.pallas_call(
        spread_kernel,
        out_shape=jax.ShapeDtypeStruct(point_traces.shape, point_traces.dtype),
        in_specs=[far] + [whole()] * 6,
        out_specs=far,
        scratch_shapes=[
            pltpu.SMEM(line, i32),
            pltpu.VMEM((tiles * step + SUBLANES, LANES), f32),
            pltpu.VMEM(((samples // LANES + 1) * step, LANES), f32),
            pltpu.VMEM((COMPS, elements) + point_traces.shape[2:], bf16),
            pltpu.SemaphoreType.DMA((COMPS + 1,)),
        ],
        compiler_params=params,
        cost_estimate=pl.CostEstimate(
            flops=2 * 192 * 96 * 3 * samples, bytes_accessed=6 << 20, transcendentals=0
        ),
        name="spread_adjoint",
    )(starts, residual, tapers, squares, other, factor, spread_weights)

    total_misfit = jnp.sum(partials[:, 0, :1], axis=0)
    return (adjoint_points, total_misfit)


def solution(mesh):
    return jax.shard_map(
        local,
        mesh=mesh,
        in_specs=(
            P(("event", "cuts"), None, None, None),
            P(("event", "cuts")),
            P(None, ("event", "cuts")),
            P(("event", "cuts"), None),
            P(("event", "cuts")),
            P(("event", "cuts")),
            P(("event", "cuts"), None, None),
        ),
        out_specs=(P(("event", "cuts"), None, None, None), P("event")),
        check_vma=False,
    )
```
